256 devices in a mesh: grp: 16 (over x_lo, z), bf: 16 (over x_hi, y, core).
Axes of the slice: x: 4 (x_hi: 2, x_lo: 2; x = x_hi * 2 + x_lo), y: 4, z: 8, core: 2. Of those that a mesh axis runs over, the one named last changes fastest.
Arguments:
- field: float32 [16, 524288], P(None, ('grp', 'bf')), may hold values from -6 to 6
- leaf_inverse: bfloat16 [1024, 512, 512], P(('grp', 'bf')), may hold values from -0.25 to 0.25
- col_factor: bfloat16 [2, 64, 524288], P(None, None, ('grp', 'bf')), may hold values from -0.125 to 0.125
- row_factor: bfloat16 [2, 64, 524288], P(None, None, ('grp', 'bf')), may hold values from -0.75 to 0.75
- mixing: bfloat16 [256, 2, 4, 2, 64, 64], P(('grp', 'bf')), may hold values from -0.5 to 0.5
- row_owner: int32 [2, 16], replicated, may hold values from 0 to 15, as said below
- rank_perm: int32 [2, 64], replicated, may hold values from 0 to 63, each once within a row
Outputs:
- applied: float32 [16, 524288], P(None, ('grp', 'bf'))
The draws below stay inside these ranges and needn't reach their ends.
Inputs may be any that keep to these rules, and one draw needn't show every extreme that they name: row_owner[l, g] = (g + s_l) mod 16; one level has s_l = 8 and the other s_l = 15, which level takes which drawn from the seed.
All inputs are finite; a program needn't handle non-finite values.
Results may differ from the reference program's by a relative error of at most 0.004.
Values sent between devices are 32-bit elements; how exact they have to be, the bound alone decides.
A program may use at most 64 MiB of HBM per device.

```python
import jax
import jax.numpy as jnp
from jax import lax

RHS = 16
K = 64
LEAF = 512
ROWS = 2048
MIXES = 4
LEVELS = 2
UNKNOWNS = 524288
N_GRP = 16
N_BF = 16


def draw_row_owner(key, part):
    key = jax.random.fold_in(key, 7)
    chosen = jax.random.randint(key, (), 0, LEVELS)
    levels = jnp.arange(LEVELS, dtype=jnp.int32)[:, None]
    shifts = jnp.where(levels == chosen, N_GRP // 2, N_GRP - 1).astype(jnp.int32)
    segments = jnp.arange(N_GRP, dtype=jnp.int32)[None, :]
    return ((segments + shifts) % N_GRP).astype(jnp.int32)


def level_of(own_key, dims, shards, least, largest):
    def one(position, blocks):
        steps = jax.random.uniform(jax.random.fold_in(jax.random.fold_in(own_key, 6), position), (blocks,), jnp.float32, least / len(shards), largest / len(shards))
        return jnp.repeat(jnp.exp(steps), dims[position] // blocks).reshape((-1,) + (1,) * (len(dims) - position - 1))

    gain = one(*shards[0])
    for cut in shards[1:]:
        gain = gain * one(*cut)
    return gain


def bell_draw(rng, shape, deviation, bound, split=(), kind=jnp.bfloat16):
    array = deviation * jax.random.normal(rng, shape, jnp.float32)
    if split:
        array = array * level_of(rng, shape, split, -0.22, 0.18)
    return jnp.clip(array, -bound, bound).astype(kind)


def setup_inputs(seed: int = 0) -> dict:
    splits = jax.random.split(jax.random.key(seed), 8)
    field = bell_draw(splits[0], (RHS, UNKNOWNS), 1.0, 6.0, ((1, 256),), jnp.float32)
    leaf_inverse = bell_draw(splits[1], (UNKNOWNS // LEAF, LEAF, LEAF), LEAF ** -0.5, 0.25, ((0, 256),))
    col_factor = bell_draw(splits[2], (LEVELS, K, UNKNOWNS), ROWS ** -0.5, 0.125, ((2, 256),))
    row_factor = bell_draw(splits[3], (LEVELS, K, UNKNOWNS), K ** -0.5, 0.75, ((2, 256),))
    mixing = bell_draw(splits[4], (N_GRP * N_BF, LEVELS, MIXES, 2, K, K), (2 * K) ** -0.5, 0.5, ((0, 256),))
    row_owner = draw_row_owner(jax.random.fold_in(splits[7], 71), 0)
    rank_perm = jax.vmap(lambda own: jax.random.permutation(own, K))(jax.random.split(splits[6], LEVELS)).reshape((LEVELS, K)).astype(jnp.int32)
    return dict(field=field, leaf_inverse=leaf_inverse, col_factor=col_factor, row_factor=row_factor, mixing=mixing, row_owner=row_owner, rank_perm=rank_perm)


def reference(field, leaf_inverse, col_factor, row_factor, mixing, row_owner, rank_perm):
    devs = N_GRP * N_BF
    hi = lax.Precision.HIGHEST
    xb = field.astype(jnp.bfloat16)
    xdev = xb.reshape(RHS, devs, ROWS).transpose(1, 0, 2)
    leaves = leaf_inverse.reshape(devs, ROWS // LEAF, LEAF, LEAF)

    def diag_one(pair):
        vec, blocks = pair
        part = vec.reshape(RHS, ROWS // LEAF, LEAF).astype(jnp.float32)
        res = jnp.einsum('rnl,nlm->rnm', part, blocks.astype(jnp.float32), precision=hi)
        return res.reshape(RHS, ROWS)

    total = lax.map(diag_one, (xdev, leaves)).reshape(N_GRP, N_BF, RHS, ROWS)
    bits = N_BF.bit_length() - 1
    index = jnp.arange(devs, dtype=jnp.int32)
    targets = jnp.arange(N_GRP, dtype=jnp.int32)
    owners_eq = (row_owner[:, None, :] == targets[None, :, None]).astype(jnp.float32)
    for level in range(LEVELS):
        vfac = col_factor[level].reshape(K, devs, ROWS).transpose(1, 0, 2)
        state = jnp.einsum('drn,dkn->drk', xdev.astype(jnp.float32), vfac.astype(jnp.float32), precision=hi)
        state = jnp.take(state, rank_perm[level], axis=2)
        for section in range(MIXES):
            bit = section % bits
            partner = jnp.bitwise_xor(index % N_BF, 1 << bit) + (index // N_BF) * N_BF
            other = state[partner]
            own_mat = mixing[:, level, section, 0].astype(jnp.float32)
            oth_mat = mixing[:, level, section, 1].astype(jnp.float32)
            state = jnp.einsum('drk,dkj->drj', state, own_mat, precision=hi) + jnp.einsum('drk,dkj->drj', other, oth_mat, precision=hi)
        rank = state.astype(jnp.bfloat16)
        rank = lax.optimization_barrier(rank).astype(jnp.float32)
        ufac = row_factor[level].reshape(K, devs, ROWS).transpose(1, 0, 2)
        out = jnp.einsum('drk,dkn->drn', rank, ufac.astype(jnp.float32), precision=hi)
        out = out.reshape(N_GRP, N_BF, RHS, ROWS)
        total = total + jnp.einsum('tg,gbrn->tbrn', owners_eq[level], out, precision=hi)
    return total.transpose(2, 0, 1, 3).reshape(RHS, N_GRP * N_BF * ROWS)
```

```python
import functools

import jax
import jax.numpy as jnp
from jax import lax
from jax.experimental import pallas as pl
from jax.experimental.pallas import tpu as pltpu
from jax.sharding import PartitionSpec as P

MESH = pl.DeviceIdType.MESH
CHUNKS = 4


def split_dot(lhs, weights):
    high = lhs.astype(jnp.bfloat16)
    low = (lhs - high.astype(jnp.float32)).astype(jnp.bfloat16)
    both = jnp.dot(
        jnp.concatenate([high, low], axis=0), weights, preferred_element_type=jnp.float32
    )
    rows = lhs.shape[0]
    return both[:rows] + both[rows:]


def kernel(
    field_hbm, leaf_hbm, col_hbm, row_hbm, mix_hbm, owner_ref, perm_ref,
    out_ref,
    field, leaf, col, row, mix, weights, own, other, outgoing, incoming,
    load_sem, leaf_sem, send_sem, recv_sem, shift_send, shift_recv,
):
    groups, width = lax.axis_size("grp"), lax.axis_size("bf")
    g, b = lax.axis_index("grp"), lax.axis_index("bf")
    vectors, rows = field.shape
    levels, rank, _ = col.shape
    leaves, order, _ = leaf.shape
    sections = mix.shape[2]
    bits = width.bit_length() - 1
    both = levels * rank

    loads = [
        pltpu.make_async_copy(src, dst, load_sem.at[i])
        for i, (src, dst) in enumerate(
            ((field_hbm, field), (col_hbm, col), (mix_hbm, mix), (row_hbm, row))
        )
    ]
    for copy in loads:
        copy.start()
    leaf_loads = [
        pltpu.make_async_copy(leaf_hbm.at[n], leaf.at[n], leaf_sem.at[n]) for n in range(leaves)
    ]
    for copy in leaf_loads:
        copy.start()

    partners = []
    for bit in range(bits):
        step = 2**bit
        partners.append(b + step - 2 * step * ((b // step) % 2))
    half = (g + groups // 2) % groups
    down, up = (g + groups - 1) % groups, (g + 1) % groups
    barrier = pltpu.get_barrier_semaphore()
    friends = [(g, p) for p in partners] + [(half, b), (down, b), (up, b)]
    for friend in friends:
        pl.semaphore_signal(barrier, inc=1, device_id=friend, device_id_type=MESH)

    loads[0].wait()
    loads[1].wait()
    xb = field[...].astype(jnp.bfloat16)
    own[0] = lax.dot_general(
        xb, col[...].reshape(both, rows), (((1,), (1,)), ((), ())),
        preferred_element_type=jnp.float32,
    )
    pl.semaphore_wait(barrier, len(friends))

    def exchange(section):
        return pltpu.make_async_remote_copy(
            src_ref=own.at[section], dst_ref=other.at[section],
            send_sem=send_sem.at[section], recv_sem=recv_sem.at[section],
            device_id=(g, partners[section % bits]), device_id_type=MESH,
        )

    def diagonal(n):
        leaf_loads[n].wait()
        out_ref[:, n * order:(n + 1) * order] = jnp.dot(
            xb[:, n * order:(n + 1) * order], leaf[n], preferred_element_type=jnp.float32
        )

    copy = exchange(0)
    copy.start()
    loads[2].wait()
    zero = jnp.zeros((rank, rank), jnp.bfloat16)
    for level in range(levels):
        index = lax.broadcasted_iota(jnp.int32, (rank, rank), 0)
        chosen = jnp.where(index == perm_ref[level:level + 1, :], 1.0, 0.0).astype(jnp.bfloat16)
        for section in range(sections):
            for part in range(2):
                block = mix[0, level, section, part]
                if section == 0:
                    block = jnp.dot(chosen, block, preferred_element_type=jnp.float32).astype(jnp.bfloat16)
                line = [zero] * levels
                line[level] = block
                start = part * both + level * rank
                weights[section, start:start + rank, :] = jnp.concatenate(line, axis=1)
    for section in range(sections):
        if section < leaves:
            diagonal(section)
        copy.wait()
        state = split_dot(
            jnp.concatenate([own[section], other[section]], axis=1), weights[section]
        )
        if section + 1 < sections:
            own[section + 1] = state
            copy = exchange(section + 1)
            copy.start()
    for n in range(sections, leaves):
        diagonal(n)

    level_of = lax.broadcasted_iota(jnp.int32, (vectors, both), 1) // rank
    half_level = jnp.where(owner_ref[0, 0] == groups // 2, 0, 1)
    pair = jnp.concatenate(
        [jnp.where(level_of == half_level, state, 0.0), jnp.where(level_of == half_level, 0.0, state)],
        axis=0,
    ).astype(jnp.bfloat16)
    loads[3].wait()
    factor = row[...].reshape(both, rows)
    size = rows // CHUNKS
    copies = []
    for c in range(CHUNKS):
        sent = jnp.dot(pair, factor[:, c * size:(c + 1) * size], preferred_element_type=jnp.float32)
        for way, target in enumerate((half, down)):
            outgoing[way, c] = sent[way * vectors:(way + 1) * vectors]
            copy = pltpu.make_async_remote_copy(
                src_ref=outgoing.at[way, c], dst_ref=incoming.at[way, c],
                send_sem=shift_send.at[way, c], recv_sem=shift_recv.at[way, c],
                device_id=(target, b), device_id_type=MESH,
            )
            copy.start()
            copies.append(copy)
    for c in range(CHUNKS):
        copies[2 * c].wait_recv()
        copies[2 * c + 1].wait_recv()
        out_ref[:, c * size:(c + 1) * size] += incoming[0, c] + incoming[1, c]
    for copy in copies:
        copy.wait_send()


def shards(field, leaf_inverse, col_factor, row_factor, mixing, row_owner, rank_perm):
    vectors, rows = field.shape
    levels, rank, _ = col_factor.shape
    sections = mixing.shape[2]
    both = levels * rank
    f32, bf16 = jnp.float32, jnp.bfloat16
    hbm = pl.BlockSpec(memory_space=pltpu.HBM)
    vmem = pl.BlockSpec(memory_space=pltpu.VMEM)
    smem = pl.BlockSpec(memory_space=pltpu.SMEM)
    return pl.pallas_call(
        kernel,
        out_shape=jax.ShapeDtypeStruct((vectors, rows), f32),
        in_specs=[hbm, hbm, hbm, hbm, hbm, smem, vmem],
        out_specs=vmem,
        scratch_shapes=[
            pltpu.VMEM(field.shape, f32),
            pltpu.VMEM(leaf_inverse.shape, bf16),
            pltpu.VMEM(col_factor.shape, bf16),
            pltpu.VMEM(row_factor.shape, bf16),
            pltpu.VMEM(mixing.shape, bf16),
            pltpu.VMEM((sections, 2 * both, both), bf16),
            pltpu.VMEM((sections, vectors, both), f32),
            pltpu.VMEM((sections, vectors, both), f32),
            pltpu.VMEM((2, CHUNKS, vectors, rows // CHUNKS), f32),
            pltpu.VMEM((2, CHUNKS, vectors, rows // CHUNKS), f32),
            pltpu.SemaphoreType.DMA((4,)),
            pltpu.SemaphoreType.DMA((leaf_inverse.shape[0],)),
            pltpu.SemaphoreType.DMA((sections,)),
            pltpu.SemaphoreType.DMA((sections,)),
            pltpu.SemaphoreType.DMA((2, CHUNKS)),
            pltpu.SemaphoreType.DMA((2, CHUNKS)),
        ],
        compiler_params=pltpu.CompilerParams(
            collective_id=0, has_side_effects=True, vmem_limit_bytes=60 * 2**20
        ),
    )(field, leaf_inverse, col_factor, row_factor, mixing, row_owner, rank_perm)


def solution(mesh):
    in_specs = (
        P(None, ("grp", "bf")),
        P(("grp", "bf"), None, None),
        P(None, None, ("grp", "bf")),
        P(None, None, ("grp", "bf")),
        P(("grp", "bf"), None, None, None, None, None),
        P(),
        P(),
    )
    out_specs = P(None, ("grp", "bf"))
    return jax.shard_map(shards, mesh=mesh, in_specs=in_specs, out_specs=out_specs, check_vma=False)
```

```python
import jax
import jax.numpy as jnp
from jax import lax
from jax.experimental import pallas as pl
from jax.experimental.pallas import tpu as pltpu
from jax.sharding import PartitionSpec as P

MESH = pl.DeviceIdType.MESH
CHUNKS = 4


def split_dot(lhs, weights):
    high = lhs.astype(jnp.bfloat16)
    low = (lhs - high.astype(jnp.float32)).astype(jnp.bfloat16)
    both = jnp.dot(
        jnp.concatenate([high, low], axis=0), weights, preferred_element_type=jnp.float32
    )
    rows = lhs.shape[0]
    return both[:rows] + both[rows:]


def flip(index, bit):
    step = 2**bit
    return index + step - 2 * step * ((index // step) % 2)


def kernel(
    field_hbm, leaf_hbm, col_hbm, row_hbm, mix_hbm, owner_hbm, perm_hbm,
    out_ref,
    field, leaf, col, row, mix, owner, perm, weights, lent, borrowed, mail, box, outgoing, incoming,
    load_sem, leaf_sem, lend_sem, mail_send, mail_recv, shift_send, shift_recv,
):
    g, b = lax.axis_index("grp"), lax.axis_index("bf")
    groups = lax.axis_size("grp")
    vectors, rows = field.shape
    levels, rank, _ = col.shape
    leaves, order, _ = leaf.shape
    sections = mix.shape[2]
    both = levels * rank

    def load(i, src, dst):
        copy = pltpu.make_async_copy(src, dst, load_sem.at[i])
        copy.start()
        return copy

    field_load = load(0, field_hbm, field)
    col_load = load(1, col_hbm, col)
    perm_load = load(2, perm_hbm, perm)
    mix_load = load(3, mix_hbm, mix)
    row_load = load(4, row_hbm, row)
    owner_load = load(5, owner_hbm, owner)
    leaf_loads = [
        pltpu.make_async_copy(leaf_hbm.at[n], leaf.at[n], leaf_sem.at[n]) for n in range(leaves)
    ]
    for copy in leaf_loads:
        copy.start()

    line, z = groups // 2, g % (groups // 2)
    half = (g + line) % groups
    down = g - z + (z + line - 1) % line
    up = g - z + (z + 1) % line
    first, second, third, fourth = (flip(b, bit) for bit in range(4))
    cross = flip(second, 2)
    friends = [(g, p) for p in (first, second, third, fourth, cross)]
    friends += [(half, b), (down, b), (up, b)]
    barrier = pltpu.get_barrier_semaphore()
    for friend in friends:
        pl.semaphore_signal(barrier, inc=1, device_id=friend, device_id_type=MESH)

    def post(slot, target):
        copy = pltpu.make_async_remote_copy(
            src_ref=mail.at[slot], dst_ref=box.at[slot],
            send_sem=mail_send.at[slot], recv_sem=mail_recv.at[slot],
            device_id=(g, target), device_id_type=MESH,
        )
        copy.start()
        return copy

    def diagonal(n):
        leaf_loads[n].wait()
        out_ref[:, n * order:(n + 1) * order] = jnp.dot(
            xb[:, n * order:(n + 1) * order], leaf[n], preferred_element_type=jnp.float32
        )

    zero = jnp.zeros((rank, rank), jnp.bfloat16)

    def blocks(index, part, made):
        for level in range(levels):
            line = [zero] * levels
            line[level] = made(level)
            start = part * both + level * rank
            weights[index, start:start + rank, :] = jnp.concatenate(line, axis=1)

    def factors(section, part):
        blocks(section, part, lambda level: mix[0, level, section, part])

    field_load.wait()
    col_load.wait()
    xb = field[...].astype(jnp.bfloat16)
    mail[0] = lax.dot_general(
        xb, col[...].reshape(both, rows), (((1,), (1,)), ((), ())),
        preferred_element_type=jnp.float32,
    )
    mix_load.wait()
    lent[...] = jnp.concatenate([mix[0, level, 1, 1] for level in range(levels)], axis=1).astype(jnp.float32)
    pl.semaphore_wait(barrier, len(friends))
    start = post(0, first)
    loan = pltpu.make_async_remote_copy(
        src_ref=lent, dst_ref=borrowed, send_sem=lend_sem.at[0], recv_sem=lend_sem.at[1],
        device_id=(g, second), device_id_type=MESH,
    )
    loan.start()
    perm_load.wait()
    index = lax.broadcasted_iota(jnp.int32, (rank, rank), 0)
    for part in range(2):
        blocks(0, part, lambda level: jnp.dot(
            jnp.where(index == perm[level:level + 1, :], 1.0, 0.0).astype(jnp.bfloat16),
            mix[0, level, 0, part], preferred_element_type=jnp.float32,
        ).astype(jnp.bfloat16))
    factors(1, 0)
    start.wait_recv()
    state = split_dot(jnp.concatenate([mail[0], box[0]], axis=1), weights[0])

    mail[1] = state
    raw = post(1, second)
    mine = split_dot(state, weights[1, :both])
    mail[2] = mine
    direct = post(2, third)
    factors(1, 1)
    factors(2, 0)
    factors(2, 1)
    loan.wait_recv()
    blocks(sections, 0, lambda level: borrowed[:, level * rank:(level + 1) * rank].astype(jnp.bfloat16))
    mail[3] = split_dot(state, weights[sections, :both])
    detour = post(3, cross)
    factors(3, 0)
    factors(3, 1)
    diagonal(0)
    diagonal(1)
    raw.wait_recv()
    state = mine + split_dot(box[1], weights[1, both:])
    mine = split_dot(state, weights[2, :both])
    detour.wait_recv()
    direct.wait_recv()
    state = mine + split_dot(box[2] + box[3], weights[2, both:])

    mail[4] = state
    last = post(4, fourth)
    mine = split_dot(state, weights[3, :both])
    for n in range(2, leaves):
        diagonal(n)
    row_load.wait()
    owner_load.wait()
    level_of = lax.broadcasted_iota(jnp.int32, (vectors, both), 1) // rank
    half_level = jnp.where(owner[0:1, 0:1] == line, 0, 1)
    to_half = level_of == half_level
    last.wait_recv()
    state = mine + split_dot(box[4], weights[3, both:])

    pair = jnp.concatenate(
        [jnp.where(to_half, state, 0.0), jnp.where(to_half, 0.0, state)], axis=0
    ).astype(jnp.bfloat16)
    factor = row[...].reshape(both, rows)
    size = rows // CHUNKS

    def shift(way, c):
        return pltpu.make_async_remote_copy(
            src_ref=outgoing.at[way, c], dst_ref=incoming.at[way, c],
            send_sem=shift_send.at[way, c], recv_sem=shift_recv.at[way, c],
            device_id=((half, down)[way], b), device_id_type=MESH,
        )

    for c in range(CHUNKS):
        sent = jnp.dot(pair, factor[:, c * size:(c + 1) * size], preferred_element_type=jnp.float32)
        outgoing[0, c] = sent[:vectors]
        outgoing[1, c] = sent[vectors:]
        shift(1, c).start()

        @pl.when(z != line - 1)
        def _():
            shift(0, c).start()

    @pl.when(z == line - 1)
    def _():
        for c in range(CHUNKS):
            shift(1, c).wait_recv()
            outgoing[0, c] += incoming[1, c]
            shift(0, c).start()

    for c in range(CHUNKS):
        where = slice(c * size, (c + 1) * size)
        shift(0, c).wait_recv()

        @pl.when(z == line - 1)
        def _():
            out_ref[:, where] += incoming[0, c]

        @pl.when(z != line - 1)
        def _():
            shift(1, c).wait_recv()
            out_ref[:, where] += incoming[0, c] + incoming[1, c]

    for copy in (start, loan, raw, direct, detour, last):
        copy.wait_send()
    for c in range(CHUNKS):
        for way in range(2):
            shift(way, c).wait_send()


def shards(field, leaf_inverse, col_factor, row_factor, mixing, row_owner, rank_perm):
    vectors, rows = field.shape
    levels, rank, _ = col_factor.shape
    sections = mixing.shape[2]
    both = levels * rank
    f32, bf16 = jnp.float32, jnp.bfloat16
    args = (field, leaf_inverse, col_factor, row_factor, mixing, row_owner, rank_perm)
    args = [pltpu.with_memory_space_constraint(x, pltpu.HBM) for x in args]
    return pl.pallas_call(
        kernel,
        out_shape=pltpu.VMEM((vectors, rows), f32),
        in_specs=[pl.BlockSpec(memory_space=pltpu.HBM)] * len(args),
        out_specs=pl.BlockSpec(memory_space=pltpu.VMEM),
        scratch_shapes=[
            pltpu.VMEM(field.shape, f32),
            pltpu.VMEM(leaf_inverse.shape, bf16),
            pltpu.VMEM(col_factor.shape, bf16),
            pltpu.VMEM(row_factor.shape, bf16),
            pltpu.VMEM(mixing.shape, bf16),
            pltpu.VMEM(row_owner.shape, jnp.int32),
            pltpu.VMEM(rank_perm.shape, jnp.int32),
            pltpu.VMEM((sections + 1, 2 * both, both), bf16),
            pltpu.VMEM((rank, both), f32),
            pltpu.VMEM((rank, both), f32),
            pltpu.VMEM((5, vectors, both), f32),
            pltpu.VMEM((5, vectors, both), f32),
            pltpu.VMEM((2, CHUNKS, vectors, rows // CHUNKS), f32),
            pltpu.VMEM((2, CHUNKS, vectors, rows // CHUNKS), f32),
            pltpu.SemaphoreType.DMA((6,)),
            pltpu.SemaphoreType.DMA((leaf_inverse.shape[0],)),
            pltpu.SemaphoreType.DMA((2,)),
            pltpu.SemaphoreType.DMA((5,)),
            pltpu.SemaphoreType.DMA((5,)),
            pltpu.SemaphoreType.DMA((2, CHUNKS)),
            pltpu.SemaphoreType.DMA((2, CHUNKS)),
        ],
        compiler_params=pltpu.CompilerParams(
            collective_id=0, has_side_effects=True, vmem_limit_bytes=60 * 2**20
        ),
    )(*args)


def solution(mesh):
    in_specs = (
        P(None, ("grp", "bf")),
        P(("grp", "bf"), None, None),
        P(None, None, ("grp", "bf")),
        P(None, None, ("grp", "bf")),
        P(("grp", "bf"), None, None, None, None, None),
        P(),
        P(),
    )
    out_specs = P(None, ("grp", "bf"))
    return jax.shard_map(shards, mesh=mesh, in_specs=in_specs, out_specs=out_specs, check_vma=False)
```

```python
import jax
import jax.numpy as jnp
from jax import lax
from jax.experimental import pallas as pl
from jax.experimental.pallas import tpu as pltpu
from jax.sharding import PartitionSpec as P

MESH = pl.DeviceIdType.MESH
CHUNKS = 4
RAW, DIRECT, DETOUR, LAST = range(4)


def split_dot(lhs, weights):
    high = lhs.astype(jnp.bfloat16)
    low = (lhs - high.astype(jnp.float32)).astype(jnp.bfloat16)
    both = jnp.dot(
        jnp.concatenate([high, low], axis=0), weights, preferred_element_type=jnp.float32
    )
    rows = lhs.shape[0]
    return both[:rows] + both[rows:]


def flip(index, bit):
    step = 2**bit
    return index + step - 2 * step * ((index // step) % 2)


def kernel(
    field_hbm, leaf_hbm, col_hbm, row_hbm, mix_hbm, owner_hbm, perm_hbm,
    out_ref,
    field, leaf, col, row, mix, owner, perm, weights,
    seed_out, seed_in, gift_out, gift_in, lent, borrowed, mail_out, mail_in,
    word_out, word_in, rows_out, rows_in, rows_low, outgoing, incoming, relay,
    load_sem, leaf_sem, seed_sem, gift_send, gift_recv, lend_send, lend_recv, mail_send, mail_recv,
    word_send, word_recv, rows_send, rows_recv, shift_send, shift_recv, relay_send, relay_recv, ready,
):
    g, b = lax.axis_index("grp"), lax.axis_index("bf")
    groups = lax.axis_size("grp")
    vectors, rows = field.shape
    levels, rank, _ = col.shape
    leaves, order, _ = leaf.shape
    sections = mix.shape[2]
    both = levels * rank
    size = rows // CHUNKS
    f32, bf16 = jnp.float32, jnp.bfloat16

    def load(i, src, dst):
        copy = pltpu.make_async_copy(src, dst, load_sem.at[i])
        copy.start()
        return copy

    mix_load = load(3, mix_hbm, mix)
    field_load = load(0, field_hbm, field)
    col_load = load(1, col_hbm, col)
    perm_load = load(2, perm_hbm, perm)
    owner_load = load(5, owner_hbm, owner)
    row_load = load(4, row_hbm, row)
    leaf_loads = [
        pltpu.make_async_copy(leaf_hbm.at[n], leaf.at[n], leaf_sem.at[n]) for n in range(leaves)
    ]
    for copy in leaf_loads:
        copy.start()

    line, core = groups // 2, b % 2
    z = g % line
    half, down, up = (g + line) % groups, g - z + (z + line - 1) % line, g - z + (z + 1) % line
    sibling, second, third, fourth = (flip(b, bit) for bit in range(4))
    cross = flip(second, 2)
    bottom, top = z == 0, z == line - 1
    barrier = pltpu.get_barrier_semaphore()

    def greet(group, member):
        pl.semaphore_signal(barrier, inc=1, device_id=(group, member), device_id_type=MESH)

    def meet(count, below, above):
        pl.semaphore_wait(
            barrier, count + below * jnp.where(bottom, 0, 1) + above * jnp.where(top, 1, 0)
        )

    greet(g, sibling)
    greet(half, b)

    @pl.when(jnp.logical_not(top))
    def _():
        greet(up, b)

    @pl.when(bottom)
    def _():
        greet(down, b + 1 - core)

    def remote(src, dst, send, recv, group, member):
        return pltpu.make_async_remote_copy(
            src_ref=src, dst_ref=dst, send_sem=send, recv_sem=recv,
            device_id=(group, member), device_id_type=MESH,
        )

    seed = remote(seed_out, seed_in, seed_sem.at[0], seed_sem.at[1], g, sibling)
    gifts = [
        remote(gift_out.at[i], gift_in.at[i], gift_send.at[i], gift_recv.at[i], g, sibling)
        for i in range(sections)
    ]

    def lend(j, member):
        return remote(lent, borrowed.at[j], lend_send.at[0], lend_recv.at[j], g, member)

    def shift(way, c):
        return remote(
            outgoing.at[way, c], incoming.at[way, c], shift_send.at[way, c], shift_recv.at[way, c],
            (half, down)[way], b,
        )

    def inward(c, member):
        return remote(
            outgoing.at[1, c], relay.at[c], shift_send.at[1, c], relay_recv.at[c], down, member
        )

    def onward(c):
        return remote(
            relay.at[c], incoming.at[1, c], relay_send.at[c], shift_recv.at[1, c], half, sibling
        )

    def word(i, group, member):
        return remote(word_out.at[i], word_in.at[i], word_send.at[i], word_recv.at[i], group, member)

    def give_rows(way):
        return remote(
            rows_out.at[way], rows_in.at[way], rows_send.at[way], rows_recv.at[way],
            (half, down)[way], b,
        )

    def joined(section, part):
        return jnp.concatenate([mix[0, level, section, part] for level in range(levels)], axis=1)

    def project():
        field_load.wait()
        col_load.wait()
        return lax.dot_general(
            field[...].astype(bf16), col[...].reshape(both, rows), (((1,), (1,)), ((), ())),
            preferred_element_type=f32,
        )

    def diagonal(n):
        leaf_loads[n].wait()
        where = slice(n * order, (n + 1) * order)
        out_ref[:, where] = jnp.dot(
            field[:, where].astype(bf16), leaf[n], preferred_element_type=f32
        )

    @pl.when(core == 0)
    def _():
        greet(half, sibling)

        @pl.when(jnp.logical_not(top))
        def _():
            greet(up, sibling)

        mix_load.wait()
        for part in range(2):
            gift_out[0, part] = joined(0, part).astype(f32)
        lent[...] = joined(1, 1).astype(f32)
        seed_out[...] = project()
        meet(3, 1, 0)
        seed.start()
        gifts[0].start()
        loan = lend(0, flip(second, 0))
        loan.start()
        for section in range(1, sections):
            for part in range(2):
                gift_out[section, part] = joined(section, part).astype(f32)
            gifts[section].start()
        perm_load.wait()
        row_load.wait()
        owner_load.wait()
        swapped = jnp.broadcast_to(owner[0:1, 0:1], (rank, rows)) != line
        rows_out[0] = jnp.where(swapped, row[1].astype(f32), row[0].astype(f32))
        give_rows(0).start()
        rows_out[1] = jnp.where(swapped, row[0].astype(f32), row[1].astype(f32))

        @pl.when(jnp.logical_not(bottom))
        def _():
            give_rows(1).start()

        for n in range(leaves):
            diagonal(n)

        @pl.when(bottom)
        def _():
            word(2, g, b).wait_recv()
            sent = word_in[2].astype(bf16)
            pl.semaphore_wait(ready, 1)
            for c in range(CHUNKS):
                outgoing[1, c] = jnp.dot(
                    sent, row[...].reshape(both, rows)[:, c * size:(c + 1) * size],
                    preferred_element_type=f32,
                )
                inward(c, sibling).start()

        give_rows(0).wait_recv()
        rows_low[:rank] = rows_in[0].astype(bf16)

        @pl.when(top)
        def _():
            rows_low[rank:] = jnp.zeros((rank, rows), bf16)
            for c in range(CHUNKS):
                shift(1, c).wait_recv()
                out_ref[:, c * size:(c + 1) * size] += incoming[1, c]
            word(0, g, b).wait_recv()
            word_in[1] = jnp.zeros((vectors, both), f32)

        @pl.when(jnp.logical_not(top))
        def _():
            give_rows(1).wait_recv()
            rows_low[rank:] = rows_in[1].astype(bf16)
            word(0, g, b).wait_recv()
            word(1, g, b).wait_recv()

        final = (word_in[0] + word_in[1]).astype(bf16)
        for c in range(CHUNKS):
            where = slice(c * size, (c + 1) * size)
            out_ref[:, where] += jnp.dot(final, rows_low[:, where], preferred_element_type=f32)

        seed.wait_send()
        for gift in gifts:
            gift.wait_send()
        loan.wait_send()
        give_rows(0).wait_send()

        @pl.when(jnp.logical_not(bottom))
        def _():
            give_rows(1).wait_send()

        @pl.when(bottom)
        def _():
            for c in range(CHUNKS):
                inward(c, sibling).wait_send()

    @pl.when(core == 1)
    def _():
        greet(g, flip(second, 0))
        for friend in (second, third, fourth, cross):
            greet(g, friend)

        zero = jnp.zeros((rank, rank), bf16)

        def place(j, section, part, made):
            for level in range(levels):
                wide = [zero] * levels
                wide[level] = made(level)
                start = part * both + level * rank
                weights[j, section, start:start + rank, :] = jnp.concatenate(wide, axis=1)

        def gift_of(section, part):
            return lambda level: gift_in[section, part, :, level * rank:(level + 1) * rank].astype(bf16)

        def mix_of(section, part):
            return lambda level: mix[0, level, section, part]

        def reordered(made):
            index = lax.broadcasted_iota(jnp.int32, (rank, rank), 0)
            return lambda level: jnp.dot(
                jnp.where(index == perm[level:level + 1, :], 1.0, 0.0).astype(bf16), made(level),
                preferred_element_type=f32,
            ).astype(bf16)

        def post(slot, target):
            return remote(
                mail_out.at[slot], mail_in.at[slot], mail_send.at[slot], mail_recv.at[slot], g, target
            )

        own = project()
        mix_load.wait()
        lent[...] = joined(1, 1).astype(f32)
        meet(7, 2, 2)

        @pl.when(top)
        def _():
            for member in (b, sibling):
                pl.semaphore_signal(ready, inc=1, device_id=(up, member), device_id_type=MESH)

        loan = lend(1, second)
        loan.start()
        perm_load.wait()
        for part in range(2):
            place(1, 0, part, reordered(mix_of(0, part)))
        place(1, 1, 0, mix_of(1, 0))
        gifts[0].wait_recv()
        for part in range(2):
            place(0, 0, part, reordered(gift_of(0, part)))
        seed.wait_recv()
        pair = [seed_in[...], own]
        state = [
            split_dot(jnp.concatenate([pair[j], pair[1 - j]], axis=1), weights[j, 0]) for j in range(2)
        ]

        for j in range(2):
            mail_out[RAW, j] = state[j]
        raw = post(RAW, second)
        raw.start()
        gifts[1].wait_recv()
        place(0, 1, 0, gift_of(1, 0))
        mine = [split_dot(state[j], weights[j, 1, :both]) for j in range(2)]
        for j in range(2):
            mail_out[DIRECT, j] = mine[j]
        direct = post(DIRECT, third)
        direct.start()
        for j in range(2):
            lend(j, b).wait_recv()
            place(j, sections, 0, lambda level: borrowed[j, :, level * rank:(level + 1) * rank].astype(bf16))
        for j in range(2):
            mail_out[DETOUR, j] = split_dot(state[j], weights[j, sections, :both])
        detour = post(DETOUR, cross)
        detour.start()
        place(0, 1, 1, gift_of(1, 1))
        place(1, 1, 1, mix_of(1, 1))
        for section in (2, 3):
            gifts[section].wait_recv()
            for part in range(2):
                place(0, section, part, gift_of(section, part))
                place(1, section, part, mix_of(section, part))
        diagonal(0)
        diagonal(1)
        raw.wait_recv()
        state = [mine[j] + split_dot(mail_in[RAW, j], weights[j, 1, both:]) for j in range(2)]
        mine = [split_dot(state[j], weights[j, 2, :both]) for j in range(2)]
        detour.wait_recv()
        direct.wait_recv()
        state = [
            mine[j] + split_dot(mail_in[DIRECT, j] + mail_in[DETOUR, j], weights[j, 2, both:])
            for j in range(2)
        ]
        for j in range(2):
            mail_out[LAST, j] = state[j]
        last = post(LAST, fourth)
        last.start()
        mine = [split_dot(state[j], weights[j, 3, :both]) for j in range(2)]
        for n in range(2, leaves):
            diagonal(n)
        row_load.wait()
        owner_load.wait()
        lane_level = lax.broadcasted_iota(jnp.int32, (vectors, both), 1) // rank
        swapped = jnp.broadcast_to(owner[0:1, 0:1], (vectors, both)) != line
        to_half = lane_level == jnp.where(swapped, 1, 0)
        last.wait_recv()
        state = [mine[j] + split_dot(mail_in[LAST, j], weights[j, 3, both:]) for j in range(2)]

        told = state[0].astype(bf16).astype(f32)
        ordered = jnp.where(swapped, pltpu.roll(told, rank, 1), told)
        word_out[0] = jnp.where(lane_level == 0, ordered, 0.0)
        word(0, half, sibling).start()

        @pl.when(bottom)
        def _():
            word_out[2] = jnp.where(to_half, 0.0, told)
            word(2, g, sibling).start()

        @pl.when(jnp.logical_not(bottom))
        def _():
            word_out[1] = jnp.where(lane_level == 0, 0.0, ordered)
            word(1, down, sibling).start()

        sent = jnp.concatenate(
            [jnp.where(to_half, state[1], 0.0), jnp.where(to_half, 0.0, state[1])], axis=0
        ).astype(bf16)
        factor = row[...].reshape(both, rows)

        @pl.when(bottom)
        def _():
            pl.semaphore_wait(ready, 1)

        for c in range(CHUNKS):
            where = slice(c * size, (c + 1) * size)
            block = jnp.dot(sent, factor[:, where], preferred_element_type=f32)
            outgoing[0, c] = block[:vectors]
            outgoing[1, c] = block[vectors:]
            shift(1, c).start()

            @pl.when(jnp.logical_not(top))
            def _():
                shift(0, c).start()

        @pl.when(top)
        def _():
            for c in range(CHUNKS):
                shift(1, c).wait_recv()
                outgoing[0, c] += incoming[1, c]
                shift(0, c).start()
            for c in range(CHUNKS):
                inward(c, b).wait_recv()
                onward(c).start()

        for c in range(CHUNKS):
            where = slice(c * size, (c + 1) * size)
            shift(0, c).wait_recv()

            @pl.when(top)
            def _():
                out_ref[:, where] += incoming[0, c]

            @pl.when(jnp.logical_not(top))
            def _():
                shift(1, c).wait_recv()
                out_ref[:, where] += incoming[0, c] + incoming[1, c]

        for copy in (loan, raw, direct, detour, last):
            copy.wait_send()
        word(0, half, sibling).wait_send()

        @pl.when(bottom)
        def _():
            word(2, g, sibling).wait_send()

        @pl.when(jnp.logical_not(bottom))
        def _():
            word(1, down, sibling).wait_send()

        for c in range(CHUNKS):
            for way in range(2):
                shift(way, c).wait_send()

        @pl.when(top)
        def _():
            for c in range(CHUNKS):
                onward(c).wait_send()


def shards(field, leaf_inverse, col_factor, row_factor, mixing, row_owner, rank_perm):
    vectors, rows = field.shape
    levels, rank, _ = col_factor.shape
    sections = mixing.shape[2]
    both = levels * rank
    f32, bf16 = jnp.float32, jnp.bfloat16
    args = (field, leaf_inverse, col_factor, row_factor, mixing, row_owner, rank_perm)
    args = [pltpu.with_memory_space_constraint(x, pltpu.HBM) for x in args]
    dma = pltpu.SemaphoreType.DMA
    return pl.pallas_call(
        kernel,
        out_shape=pltpu.VMEM((vectors, rows), f32),
        in_specs=[pl.BlockSpec(memory_space=pltpu.HBM)] * len(args),
        out_specs=pl.BlockSpec(memory_space=pltpu.VMEM),
        scratch_shapes=[
            pltpu.VMEM(field.shape, f32),
            pltpu.VMEM(leaf_inverse.shape, bf16),
            pltpu.VMEM(col_factor.shape, bf16),
            pltpu.VMEM(row_factor.shape, bf16),
            pltpu.VMEM(mixing.shape, bf16),
            pltpu.VMEM(row_owner.shape, jnp.int32),
            pltpu.VMEM(rank_perm.shape, jnp.int32),
            pltpu.VMEM((2, sections + 1, 2 * both, both), bf16),
            pltpu.VMEM((vectors, both), f32),
            pltpu.VMEM((vectors, both), f32),
            pltpu.VMEM((sections, 2, rank, both), f32),
            pltpu.VMEM((sections, 2, rank, both), f32),
            pltpu.VMEM((rank, both), f32),
            pltpu.VMEM((2, rank, both), f32),
            pltpu.VMEM((4, 2, vectors, both), f32),
            pltpu.VMEM((4, 2, vectors, both), f32),
            pltpu.VMEM((3, vectors, both), f32),
            pltpu.VMEM((3, vectors, both), f32),
            pltpu.VMEM((2, rank, rows), f32),
            pltpu.VMEM((2, rank, rows), f32),
            pltpu.VMEM((both, rows), bf16),
            pltpu.VMEM((2, CHUNKS, vectors, rows // CHUNKS), f32),
            pltpu.VMEM((2, CHUNKS, vectors, rows // CHUNKS), f32),
            pltpu.VMEM((CHUNKS, vectors, rows // CHUNKS), f32),
            dma((6,)), dma((leaf_inverse.shape[0],)), dma((2,)), dma((sections,)), dma((sections,)),
            dma((1,)), dma((2,)), dma((4,)), dma((4,)), dma((3,)), dma((3,)), dma((2,)), dma((2,)),
            dma((2, CHUNKS)), dma((2, CHUNKS)), dma((CHUNKS,)), dma((CHUNKS,)),
            pltpu.SemaphoreType.REGULAR,
        ],
        compiler_params=pltpu.CompilerParams(
            collective_id=0, has_side_effects=True, vmem_limit_bytes=60 * 2**20
        ),
    )(*args)


def solution(mesh):
    in_specs = (
        P(None, ("grp", "bf")),
        P(("grp", "bf"), None, None),
        P(None, None, ("grp", "bf")),
        P(None, None, ("grp", "bf")),
        P(("grp", "bf"), None, None, None, None, None),
        P(),
        P(),
    )
    out_specs = P(None, ("grp", "bf"))
    return jax.shard_map(shards, mesh=mesh, in_specs=in_specs, out_specs=out_specs, check_vma=False)
```

```python
import jax
import jax.numpy as jnp
from jax import lax
from jax.experimental import pallas as pl
from jax.experimental.pallas import tpu as pltpu
from jax.sharding import PartitionSpec as P

MESH = pl.DeviceIdType.MESH
AHEAD = 3, 8
PIECES = 2
RAW, DIRECT, DETOUR, LAST = range(4)
GIFTS = ((1, 1), (0, 0), (0, 1), (1, 0), (2, 0), (2, 1), (3, 0), (3, 1))


def split_dot(lhs, weights):
    high = lhs.astype(jnp.bfloat16)
    low = (lhs - high.astype(jnp.float32)).astype(jnp.bfloat16)
    both = jnp.dot(
        jnp.concatenate([high, low], axis=0), weights, preferred_element_type=jnp.float32
    )
    rows = lhs.shape[0]
    return both[:rows] + both[rows:]


def flip(index, bit):
    step = 2**bit
    return index + step - 2 * step * ((index // step) % 2)


def kernel(
    field_hbm, leaf_hbm, col_hbm, row_hbm, mix_hbm, owner_hbm, perm_hbm,
    out_ref,
    field, leaf, col, row, mix, owner, perm, weights,
    seed_out, seed_in, gift_out, gift_in, lent, borrowed, mail_out, mail_in,
    word_out, word_in, rows_out, rows_in, ahead_out, ahead_held, ahead_in, rows_low,
    out_first, out_rest, in_first, in_rest, relay_first, relay_rest,
    load_sem, leaf_sem, seed_sem, gift_send, gift_recv, lend_send, lend_recv, mail_send, mail_recv,
    word_send, word_recv, rows_send, rows_recv, held_send, held_recv, ahead_send, ahead_recv, shift_send, shift_recv, relay_send, relay_recv, ready, go,
):
    g, b = lax.axis_index("grp"), lax.axis_index("bf")
    groups = lax.axis_size("grp")
    vectors, rows = field.shape
    levels, rank, _ = col.shape
    leaves, order, _ = leaf.shape
    sections = mix.shape[2]
    both = levels * rank
    ahead = out_first.shape[2]
    pieces = (slice(0, ahead), slice(ahead, rows))
    outgoing, incoming, relay = (out_first, out_rest), (in_first, in_rest), (relay_first, relay_rest)
    f32, bf16 = jnp.float32, jnp.bfloat16

    def load(i, src, dst):
        copy = pltpu.make_async_copy(src, dst, load_sem.at[i])
        copy.start()
        return copy

    half_mix = sections // 2
    mix_load = load(3, mix_hbm.at[:, :, :half_mix], mix.at[:, :, :half_mix])
    perm_load = load(2, perm_hbm, perm)
    field_load = load(0, field_hbm, field)
    col_load = load(1, col_hbm, col)
    rest_load = load(6, mix_hbm.at[:, :, half_mix:], mix.at[:, :, half_mix:])

    line, core = groups // 2, b % 2
    z = g % line
    half, down, up = (g + line) % groups, g - z + (z + line - 1) % line, g - z + (z + 1) % line
    sibling, second, third, fourth = (flip(b, bit) for bit in range(4))
    cross = flip(second, 2)
    bottom, top = z == 0, z == line - 1
    barrier = pltpu.get_barrier_semaphore()

    def greet(group, member):
        pl.semaphore_signal(barrier, inc=1, device_id=(group, member), device_id_type=MESH)

    greet(g, sibling)
    greet(half, b + 1 - core)

    @pl.when(jnp.logical_not(top))
    def _():
        greet(up, b + 1 - core)

    @pl.when(bottom)
    def _():
        greet(down, b + 1 - core)

    @pl.when(core == 1)
    def _():
        for friend in (third, fourth, second, cross):
            greet(g, friend)

    owner_load = load(5, owner_hbm, owner)
    row_load = load(4, row_hbm, row)
    leaf_loads = [
        pltpu.make_async_copy(leaf_hbm.at[n], leaf.at[n], leaf_sem.at[n]) for n in range(leaves)
    ]
    for copy in leaf_loads:
        copy.start()

    def remote(src, dst, send, recv, group, member):
        return pltpu.make_async_remote_copy(
            src_ref=src, dst_ref=dst, send_sem=send, recv_sem=recv,
            device_id=(group, member), device_id_type=MESH,
        )

    seed = remote(seed_out, seed_in, seed_sem.at[0], seed_sem.at[1], g, sibling)
    gifts = [
        remote(gift_out.at[part], gift_in.at[part], gift_send.at[i], gift_recv.at[i], g, sibling)
        for i, part in enumerate((pl.ds(0, 4), pl.ds(4, 4)))
    ]

    def lend(j, source):
        return remote(source, borrowed.at[j], lend_send.at[j], lend_recv.at[j], g, third)

    def shift(way, c):
        return remote(
            outgoing[c].at[way], incoming[c].at[way], shift_send.at[way, c], shift_recv.at[way, c],
            (half, down)[way], b,
        )

    def inward(c, member):
        return remote(
            outgoing[c].at[1], relay[c], shift_send.at[1, c], relay_recv.at[c], down, member
        )

    def onward(c):
        return remote(
            relay[c], incoming[c].at[1], relay_send.at[c], shift_recv.at[1, c], half, sibling
        )

    def word(i, group, member):
        return remote(word_out.at[i], word_in.at[i], word_send.at[i], word_recv.at[i], group, member)

    def give_rows(way):
        return remote(
            rows_out.at[way], rows_in.at[way], rows_send.at[way], rows_recv.at[way],
            (half, down)[way], b,
        )

    def hold(way):
        return remote(
            ahead_out.at[way], ahead_held.at[way], held_send.at[way], held_recv.at[way], g, sibling
        )

    def give_ahead(way, member):
        return remote(
            ahead_held.at[way], ahead_in.at[way], ahead_send.at[way], ahead_recv.at[way],
            (half, down)[way], member,
        )

    def by_way(width):
        swapped = jnp.broadcast_to(owner[0:1, 0:1], (rank, width)) != line
        first, other = row[0, :, :width].astype(f32), row[1, :, :width].astype(f32)
        return jnp.where(swapped, other, first), jnp.where(swapped, first, other)

    def factor_of(section, part):
        def made(level):
            block = mix[0, level, section, part]
            if section:
                return block
            index = lax.broadcasted_iota(jnp.int32, (rank, rank), 0)
            chosen = jnp.where(index == perm[level:level + 1, :], 1.0, 0.0).astype(bf16)
            return jnp.dot(chosen, block, preferred_element_type=f32).astype(bf16)

        return made

    def joined(section, part):
        made = factor_of(section, part)
        return jnp.concatenate([made(level) for level in range(levels)], axis=1).astype(f32)

    def project():
        field_load.wait()
        col_load.wait()
        return lax.dot_general(
            field[...].astype(bf16), col[...].reshape(both, rows), (((1,), (1,)), ((), ())),
            preferred_element_type=f32,
        )

    def diagonal(n):
        leaf_loads[n].wait()
        where = slice(n * order, (n + 1) * order)
        out_ref[:, where] = jnp.dot(
            field[:, where].astype(bf16), leaf[n], preferred_element_type=f32
        )

    @pl.when(core == 0)
    def _():
        mix_load.wait()
        perm_load.wait()
        for i, (section, part) in enumerate(GIFTS[:4]):
            gift_out[i] = joined(section, part)
        pl.semaphore_wait(barrier, 1)
        gifts[0].start()
        seed_out[...] = project()
        seed.start()
        rest_load.wait()
        for i, (section, part) in enumerate(GIFTS[4:], 4):
            gift_out[i] = joined(section, part)
        gifts[1].start()
        row_load.wait()
        owner_load.wait()
        rows_out[0], rows_out[1] = by_way(rows)

        pl.semaphore_wait(go, 1)
        give_rows(0).start()

        @pl.when(jnp.logical_not(bottom))
        def _():
            give_rows(1).start()

        @pl.when(jnp.logical_not(bottom))
        def _():
            hold(1).wait_recv()
            give_ahead(1, sibling).start()

        @pl.when(jnp.logical_not(top))
        def _():
            hold(0).wait_recv()
            give_ahead(0, sibling).start()

        for n in range(leaves):
            diagonal(n)

        @pl.when(bottom)
        def _():
            word(4, g, b).wait_recv()
            sent = word_in[4].astype(bf16)
            pl.semaphore_wait(ready, 1)
            for c, where in enumerate(pieces):
                outgoing[c][1] = jnp.dot(
                    sent, row[...].reshape(both, rows)[:, where], preferred_element_type=f32
                )
                inward(c, sibling).start()

        give_rows(0).wait_recv()
        rows_low[:rank] = rows_in[0].astype(bf16)

        @pl.when(top)
        def _():
            rows_low[rank:] = jnp.zeros((rank, rows), bf16)
            word_in[1] = jnp.zeros((vectors, both), f32)

        @pl.when(jnp.logical_not(top))
        def _():
            give_rows(1).wait_recv()
            rows_low[rank:] = rows_in[1].astype(bf16)
            word(1, g, b).wait_recv()

        word(0, g, b).wait_recv()
        final = (word_in[0] + word_in[1]).astype(bf16)
        out_ref[...] += jnp.dot(final, rows_low[...], preferred_element_type=f32)

        @pl.when(top)
        def _():
            for c, where in enumerate(pieces):
                shift(1, c).wait_recv()
                out_ref[:, where] += incoming[c][1]

        seed.wait_send()
        for gift in gifts:
            gift.wait_send()
        give_rows(0).wait_send()

        @pl.when(jnp.logical_not(bottom))
        def _():
            give_rows(1).wait_send()
            give_ahead(1, sibling).wait_send()

        @pl.when(jnp.logical_not(top))
        def _():
            give_ahead(0, sibling).wait_send()

        @pl.when(bottom)
        def _():
            for c in range(PIECES):
                inward(c, sibling).wait_send()

    @pl.when(core == 1)
    def _():
        zero = jnp.zeros((rank, rank), bf16)

        def place(j, section, part, made):
            for level in range(levels):
                wide = [zero] * levels
                wide[level] = made(level)
                start = part * both + level * rank
                weights[j, section, start:start + rank, :] = jnp.concatenate(wide, axis=1)

        def gift_of(section, part):
            i = GIFTS.index((section, part))
            return lambda level: gift_in[i, :, level * rank:(level + 1) * rank].astype(bf16)

        def post(kept, slot, target):
            return remote(
                mail_out.at[kept], mail_in.at[slot], mail_send.at[slot], mail_recv.at[slot], g, target
            )

        mix_load.wait()
        perm_load.wait()
        lent[...] = joined(1, 1)
        for part in range(2):
            place(1, 0, part, factor_of(0, part))
        place(1, 1, 0, factor_of(1, 0))
        own = project()
        pl.semaphore_wait(barrier, 7 + jnp.where(bottom, 0, 2) + jnp.where(top, 2, 0))
        loans = [lend(0, gift_in.at[0]), lend(1, lent)]
        loans[1].start()
        pl.semaphore_signal(go, inc=1, device_id=(g, sibling), device_id_type=MESH)

        @pl.when(top)
        def _():
            for member in (b, sibling):
                pl.semaphore_signal(ready, inc=1, device_id=(up, member), device_id_type=MESH)

        gifts[0].wait_recv()
        loans[0].start()
        for part in range(2):
            place(0, 0, part, gift_of(0, part))
        place(0, 1, 0, gift_of(1, 0))
        seed.wait_recv()
        pair = [seed_in[...], own]
        state = [
            split_dot(jnp.concatenate([pair[j], pair[1 - j]], axis=1), weights[j, 0]) for j in range(2)
        ]

        raw, detour = post(RAW, RAW, second), post(RAW, DETOUR, cross)
        direct = post(DIRECT, DIRECT, third)
        mine = [split_dot(state[j], weights[j, 1, :both]) for j in range(2)]
        for j in range(2):
            mail_out[RAW, j] = state[j]
            mail_out[DIRECT, j] = mine[j]
        direct.start()
        detour.start()
        raw.start()
        place(0, 1, 1, gift_of(1, 1))
        place(1, 1, 1, factor_of(1, 1))
        rest_load.wait()
        gifts[1].wait_recv()
        for section in (2, 3):
            for part in range(2):
                place(0, section, part, gift_of(section, part))
                place(1, section, part, factor_of(section, part))
        row_load.wait()
        owner_load.wait()
        ahead_out[0], ahead_out[1] = by_way(ahead)

        @pl.when(jnp.logical_not(bottom))
        def _():
            hold(1).start()

        @pl.when(jnp.logical_not(top))
        def _():
            hold(0).start()

        diagonal(0)
        diagonal(1)
        raw.wait_recv()
        state = [mine[j] + split_dot(mail_in[RAW, j], weights[j, 1, both:]) for j in range(2)]
        mine = [split_dot(state[j], weights[j, 2, :both]) for j in range(2)]
        detour.wait_recv()
        for j in range(2):
            loans[j].wait_recv()
            place(j, sections, 0, lambda level: borrowed[j, :, level * rank:(level + 1) * rank].astype(bf16))
        far = [split_dot(mail_in[DETOUR, j], weights[j, sections, :both]) for j in range(2)]
        direct.wait_recv()
        state = [
            mine[j] + split_dot(mail_in[DIRECT, j] + far[j], weights[j, 2, both:]) for j in range(2)
        ]
        for j in range(2):
            mail_out[LAST, j] = state[j]
        last = post(LAST, LAST, fourth)
        last.start()
        mine = [split_dot(state[j], weights[j, 3, :both]) for j in range(2)]
        for n in range(2, leaves):
            diagonal(n)
        lane_level = lax.broadcasted_iota(jnp.int32, (vectors, both), 1) // rank
        swapped = jnp.broadcast_to(owner[0:1, 0:1], (vectors, both)) != line
        to_half = lane_level == jnp.where(swapped, 1, 0)
        last.wait_recv()
        state = [mine[j] + split_dot(mail_in[LAST, j], weights[j, 3, both:]) for j in range(2)]

        told = [state[j].astype(bf16).astype(f32) for j in range(2)]
        ordered = [jnp.where(swapped, pltpu.roll(told[j], rank, 1), told[j]) for j in range(2)]
        for j in range(2):
            word_out[2 * j] = jnp.where(lane_level == 0, ordered[j], 0.0)
            word_out[2 * j + 1] = jnp.where(lane_level == 0, 0.0, ordered[j])
        word_out[4] = jnp.where(to_half, 0.0, told[0])
        sent = jnp.concatenate(
            [jnp.where(to_half, told[1], 0.0), jnp.where(to_half, 0.0, told[1])], axis=0
        ).astype(bf16)
        factor = row[...].reshape(both, rows)

        def make(c):
            block = jnp.dot(sent, factor[:, pieces[c]], preferred_element_type=f32)
            outgoing[c][0] = block[:vectors]
            outgoing[c][1] = block[vectors:]

        @pl.when(bottom)
        def _():
            word(4, g, sibling).start()

        @pl.when(jnp.logical_not(bottom))
        def _():
            word(1, down, sibling).start()
            word(3, down, b).start()

        word(0, half, sibling).start()

        @pl.when(jnp.logical_not(top))
        def _():
            word(2, half, b).start()

        make(1)

        @pl.when(jnp.logical_not(bottom))
        def _():
            shift(1, 1).start()

        @pl.when(jnp.logical_not(top))
        def _():
            shift(0, 1).start()

        @pl.when(bottom)
        def _():
            make(0)
            pl.semaphore_wait(ready, 1)
            for c in range(PIECES):
                shift(1, c).start()

        @pl.when(top)
        def _():
            make(0)
            for c, where in enumerate(pieces):
                shift(1, c).wait_recv()
                outgoing[c][0] += incoming[c][1]
                shift(0, c).start()
            for c in range(PIECES):
                inward(c, b).wait_recv()
                onward(c).start()
            for c, where in enumerate(pieces):
                shift(0, c).wait_recv()
                out_ref[:, where] += incoming[c][0]

        @pl.when(jnp.logical_not(top))
        def _():
            for way in (1, 0):
                give_ahead(way, b).wait_recv()
                rows_low[way * rank:(way + 1) * rank, :ahead] = ahead_in[way].astype(bf16)
                word(2 + way, g, b).wait_recv()
            final = (word_in[2] + word_in[3]).astype(bf16)
            out_ref[:, :ahead] += jnp.dot(final, rows_low[:, :ahead], preferred_element_type=f32)
            for way in (1, 0):
                shift(way, 1).wait_recv()
            out_ref[:, ahead:] += incoming[1][0] + incoming[1][1]

        for copy in (*loans, raw, direct, detour, last):
            copy.wait_send()
        word(0, half, sibling).wait_send()
        for way in range(2):
            shift(way, 1).wait_send()

        @pl.when(bottom)
        def _():
            word(4, g, sibling).wait_send()
            shift(1, 0).wait_send()

        @pl.when(jnp.logical_not(bottom))
        def _():
            hold(1).wait_send()
            word(1, down, sibling).wait_send()
            word(3, down, b).wait_send()

        @pl.when(top)
        def _():
            shift(0, 0).wait_send()
            for c in range(PIECES):
                onward(c).wait_send()

        @pl.when(jnp.logical_not(top))
        def _():
            hold(0).wait_send()
            word(2, half, b).wait_send()


def shards(field, leaf_inverse, col_factor, row_factor, mixing, row_owner, rank_perm):
    vectors, rows = field.shape
    levels, rank, _ = col_factor.shape
    sections = mixing.shape[2]
    both = levels * rank
    ahead = rows * AHEAD[0] // AHEAD[1]
    f32, bf16 = jnp.float32, jnp.bfloat16
    args = (field, leaf_inverse, col_factor, row_factor, mixing, row_owner, rank_perm)
    args = [pltpu.with_memory_space_constraint(x, pltpu.HBM) for x in args]
    dma = pltpu.SemaphoreType.DMA
    return pl.pallas_call(
        kernel,
        out_shape=pltpu.VMEM((vectors, rows), f32),
        in_specs=[pl.BlockSpec(memory_space=pltpu.HBM)] * len(args),
        out_specs=pl.BlockSpec(memory_space=pltpu.VMEM),
        scratch_shapes=[
            pltpu.VMEM(field.shape, f32),
            pltpu.VMEM(leaf_inverse.shape, bf16),
            pltpu.VMEM(col_factor.shape, bf16),
            pltpu.VMEM(row_factor.shape, bf16),
            pltpu.VMEM(mixing.shape, bf16),
            pltpu.VMEM(row_owner.shape, jnp.int32),
            pltpu.VMEM(rank_perm.shape, jnp.int32),
            pltpu.VMEM((2, sections + 1, 2 * both, both), bf16),
            pltpu.VMEM((vectors, both), f32),
            pltpu.VMEM((vectors, both), f32),
            pltpu.VMEM((2 * sections, rank, both), f32),
            pltpu.VMEM((2 * sections, rank, both), f32),
            pltpu.VMEM((rank, both), f32),
            pltpu.VMEM((2, rank, both), f32),
            pltpu.VMEM((4, 2, vectors, both), f32),
            pltpu.VMEM((4, 2, vectors, both), f32),
            pltpu.VMEM((5, vectors, both), f32),
            pltpu.VMEM((5, vectors, both), f32),
            pltpu.VMEM((2, rank, rows), f32),
            pltpu.VMEM((2, rank, rows), f32),
            pltpu.VMEM((2, rank, ahead), f32),
            pltpu.VMEM((2, rank, ahead), f32),
            pltpu.VMEM((2, rank, ahead), f32),
            pltpu.VMEM((both, rows), bf16),
            pltpu.VMEM((2, vectors, ahead), f32),
            pltpu.VMEM((2, vectors, rows - ahead), f32),
            pltpu.VMEM((2, vectors, ahead), f32),
            pltpu.VMEM((2, vectors, rows - ahead), f32),
            pltpu.VMEM((vectors, ahead), f32),
            pltpu.VMEM((vectors, rows - ahead), f32),
            dma((7,)), dma((leaf_inverse.shape[0],)), dma((2,)), dma((2,)), dma((2,)),
            dma((2,)), dma((2,)), dma((4,)), dma((4,)), dma((5,)), dma((5,)), dma((2,)), dma((2,)), dma((2,)), dma((2,)),
            dma((2,)), dma((2,)),
            dma((2, PIECES)), dma((2, PIECES)), dma((PIECES,)), dma((PIECES,)),
            pltpu.SemaphoreType.REGULAR, pltpu.SemaphoreType.REGULAR,
        ],
        compiler_params=pltpu.CompilerParams(
            collective_id=0, has_side_effects=True, vmem_limit_bytes=60 * 2**20
        ),
    )(*args)


def solution(mesh):
    in_specs = (
        P(None, ("grp", "bf")),
        P(("grp", "bf"), None, None),
        P(None, None, ("grp", "bf")),
        P(None, None, ("grp", "bf")),
        P(("grp", "bf"), None, None, None, None, None),
        P(),
        P(),
    )
    out_specs = P(None, ("grp", "bf"))
    return jax.shard_map(shards, mesh=mesh, in_specs=in_specs, out_specs=out_specs, check_vma=False)
```

```python
import jax
import jax.numpy as jnp
from jax import lax
from jax.experimental import pallas as pl
from jax.experimental.pallas import tpu as pltpu
from jax.sharding import PartitionSpec as P

MESH = pl.DeviceIdType.MESH
AHEAD = 3, 8
PIECES = 2
STRIP = 16
RAW, DIRECT, DETOUR, LAST = range(4)
GIFTS = ((1, 1), (0, 0), (0, 1), (1, 0), (2, 0), (2, 1), (3, 0), (3, 1))


def split_dot(lhs, weights):
    high = lhs.astype(jnp.bfloat16)
    low = (lhs - high.astype(jnp.float32)).astype(jnp.bfloat16)
    both = jnp.dot(
        jnp.concatenate([high, low], axis=0), weights, preferred_element_type=jnp.float32
    )
    rows = lhs.shape[0]
    return both[:rows] + both[rows:]


def flip(index, bit):
    step = 2**bit
    return index + step - 2 * step * lax.rem(lax.div(index, step), 2)


def kernel(
    field_hbm, leaf_hbm, col_hbm, row_hbm, mix_hbm, owner_hbm, perm_hbm,
    out_ref,
    field, leaf, col, row, mix, owner, perm, weights,
    seed_out, seed_in, gift_out, gift_in, lent, borrowed, mail_out, mail_in,
    word_out, word_in, rows_out, rows_in, ahead_out, ahead_held, ahead_in, rows_low,
    out_first, out_rest, in_first, in_rest, relay_first, relay_rest,
    load_sem, leaf_sem, seed_sem, gift_send, gift_recv, lend_send, lend_recv, mail_send, mail_recv,
    word_send, word_recv, rows_send, rows_recv, held_send, held_recv, ahead_send, ahead_recv, shift_send, shift_recv, relay_send, relay_recv, ready, go,
):
    g, b = lax.axis_index("grp"), lax.axis_index("bf")
    groups = lax.axis_size("grp")
    vectors, rows = field.shape
    levels, rank, _ = col.shape
    leaves, order, _ = leaf.shape
    sections = mix.shape[2]
    both = levels * rank
    ahead = out_first.shape[2]
    pieces = (slice(0, ahead), slice(ahead, rows))
    outgoing, incoming, relay = (out_first, out_rest), (in_first, in_rest), (relay_first, relay_rest)
    f32, bf16 = jnp.float32, jnp.bfloat16

    def load(i, src, dst):
        copy = pltpu.make_async_copy(src, dst, load_sem.at[i])
        copy.start()
        return copy

    line, core = groups // 2, lax.rem(b, 2)
    z = lax.rem(g, line)
    half, down, up = lax.rem(g + line, groups), g - z + lax.rem(z + line - 1, line), g - z + lax.rem(z + 1, line)
    sibling, second, third, fourth = (flip(b, bit) for bit in range(4))
    cross = flip(second, 2)
    bottom, top = z == 0, z == line - 1
    barrier = pltpu.get_barrier_semaphore()

    def greet(group, member):
        pl.semaphore_signal(barrier, inc=1, device_id=(group, member), device_id_type=MESH)

    greet(half, b + 1 - core)

    @pl.when(jnp.logical_not(top))
    def _():
        greet(up, b + 1 - core)

    @pl.when(bottom)
    def _():
        greet(down, b + 1 - core)

    @pl.when(core == 1)
    def _():
        for friend in (third, fourth, second, cross):
            greet(g, friend)

    greet(g, sibling)
    half_mix = sections // 2
    mix_load = load(3, mix_hbm.at[:, :, :half_mix], mix.at[:, :, :half_mix])
    perm_load = load(2, perm_hbm, perm)
    field_load = load(0, field_hbm, field)
    col_load = load(1, col_hbm, col)
    rest_load = load(6, mix_hbm.at[:, :, half_mix:], mix.at[:, :, half_mix:])

    owner_load = load(5, owner_hbm, owner)
    row_load = load(4, row_hbm, row)
    leaf_loads = [
        pltpu.make_async_copy(leaf_hbm.at[n], leaf.at[n], leaf_sem.at[n]) for n in range(leaves)
    ]

    def remote(src, dst, send, recv, group, member):
        return pltpu.make_async_remote_copy(
            src_ref=src, dst_ref=dst, send_sem=send, recv_sem=recv,
            device_id=(group, member), device_id_type=MESH,
        )

    seed = remote(seed_out, seed_in, seed_sem.at[0], seed_sem.at[1], g, sibling)
    gifts = [
        remote(gift_out.at[part], gift_in.at[part], gift_send.at[i], gift_recv.at[i], g, sibling)
        for i, part in enumerate((pl.ds(0, 1), pl.ds(1, 3), pl.ds(4, 4)))
    ]

    def lend(j, source):
        return remote(source, borrowed.at[j], lend_send.at[j], lend_recv.at[j], g, third)

    def shift(way, c):
        return remote(
            outgoing[c].at[way], incoming[c].at[way], shift_send.at[way, c], shift_recv.at[way, c],
            (half, down)[way], b,
        )

    def inward(c, member):
        return remote(
            outgoing[c].at[1], relay[c], shift_send.at[1, c], relay_recv.at[c], down, member
        )

    def onward(c):
        return remote(
            relay[c], incoming[c].at[1], relay_send.at[c], shift_recv.at[1, c], half, sibling
        )

    def word(i, group, member):
        return remote(word_out.at[i], word_in.at[i], word_send.at[i], word_recv.at[i], group, member)

    def give_rows(way):
        return remote(
            rows_out.at[way], rows_in.at[way], rows_send.at[way], rows_recv.at[way],
            (half, down)[way], b,
        )

    def hold(way):
        return remote(
            ahead_out.at[way], ahead_held.at[way], held_send.at[way], held_recv.at[way], g, sibling
        )

    def give_ahead(way, member):
        return remote(
            ahead_held.at[way], ahead_in.at[way], ahead_send.at[way], ahead_recv.at[way],
            (half, down)[way], member,
        )

    def by_way(into):
        width = into.shape[2]
        swapped = jnp.broadcast_to(owner[0:1, 0:1], (STRIP, width)) != line

        def strip(i, carry):
            where = pl.ds(pl.multiple_of(i * STRIP, STRIP), STRIP)
            first, other = row[0, where, :width].astype(f32), row[1, where, :width].astype(f32)
            into[0, where] = jnp.where(swapped, other, first)
            into[1, where] = jnp.where(swapped, first, other)
            return carry

        lax.fori_loop(0, rank // STRIP, strip, 0)

    def narrow(way, source, width):
        def strip(i, carry):
            where = pl.ds(pl.multiple_of(i * STRIP, STRIP), STRIP)
            into = pl.ds(pl.multiple_of(way * rank + i * STRIP, STRIP), STRIP)
            rows_low[into, :width] = source[way, where].astype(bf16)
            return carry

        lax.fori_loop(0, rank // STRIP, strip, 0)

    def factor_of(section, part):
        return lambda level: mix[0, level, section, part]

    def joined(section, part):
        return jnp.concatenate([mix[0, level, section, part] for level in range(levels)], axis=1).astype(f32)

    def project():
        field_load.wait()
        col_load.wait()
        return lax.dot_general(
            field[...].astype(bf16), col[...].reshape(both, rows), (((1,), (1,)), ((), ())),
            preferred_element_type=f32,
        )

    def diagonal(n):
        pltpu.make_async_copy(leaf_hbm.at[n], leaf.at[n], leaf_sem.at[n]).wait()
        where = pl.ds(pl.multiple_of(n * order, order), order)
        out_ref[:, where] = jnp.dot(
            field[:, where].astype(bf16), leaf[n], preferred_element_type=f32
        )

    def diagonals(start, stop):
        def one(n, carry):
            diagonal(n)
            return carry

        lax.fori_loop(start, stop, one, 0)

    @pl.when(core == 0)
    def _():
        mix_load.wait()
        gift_out[0] = joined(*GIFTS[0])
        pl.semaphore_wait(barrier, 1)
        gifts[0].start()
        for i, (section, part) in enumerate(GIFTS[1:4], 1):
            gift_out[i] = joined(section, part)
        gifts[1].start()
        seed_out[...] = project()
        seed.start()
        for copy in leaf_loads:
            copy.start()
        rest_load.wait()
        for i, (section, part) in enumerate(GIFTS[4:], 4):
            gift_out[i] = joined(section, part)
        gifts[2].start()
        perm_load.wait()
        row_load.wait()
        owner_load.wait()
        by_way(rows_out)

        pl.semaphore_wait(go, 1)
        give_rows(0).start()

        @pl.when(jnp.logical_not(bottom))
        def _():
            give_rows(1).start()

        @pl.when(jnp.logical_not(bottom))
        def _():
            hold(1).wait_recv()
            give_ahead(1, sibling).start()

        @pl.when(jnp.logical_not(top))
        def _():
            hold(0).wait_recv()
            give_ahead(0, sibling).start()

        diagonals(0, leaves)

        @pl.when(bottom)
        def _():
            word(4, g, b).wait_recv()
            sent = word_in[4].astype(bf16)
            pl.semaphore_wait(ready, 1)
            for c, where in enumerate(pieces):
                outgoing[c][1] = jnp.dot(
                    sent, row[...].reshape(both, rows)[:, where], preferred_element_type=f32
                )
                inward(c, sibling).start()

        give_rows(0).wait_recv()
        narrow(0, rows_in, rows)

        @pl.when(top)
        def _():
            rows_low[rank:] = jnp.zeros((rank, rows), bf16)
            word_in[1] = jnp.zeros((vectors, both), f32)

        @pl.when(jnp.logical_not(top))
        def _():
            give_rows(1).wait_recv()
            narrow(1, rows_in, rows)
            word(1, g, b).wait_recv()

        word(0, g, b).wait_recv()
        final = (word_in[0] + word_in[1]).astype(bf16)

        def expand(n, carry):
            where = pl.ds(pl.multiple_of(n * order, order), order)
            out_ref[:, where] += jnp.dot(final, rows_low[:, where], preferred_element_type=f32)
            return carry

        lax.fori_loop(0, leaves, expand, 0)

        @pl.when(top)
        def _():
            for c, where in enumerate(pieces):
                shift(1, c).wait_recv()
                out_ref[:, where] += incoming[c][1]

        seed.wait_send()
        for gift in gifts:
            gift.wait_send()
        give_rows(0).wait_send()

        @pl.when(jnp.logical_not(bottom))
        def _():
            give_rows(1).wait_send()
            give_ahead(1, sibling).wait_send()

        @pl.when(jnp.logical_not(top))
        def _():
            give_ahead(0, sibling).wait_send()

        @pl.when(bottom)
        def _():
            for c in range(PIECES):
                inward(c, sibling).wait_send()

    @pl.when(core == 1)
    def _():
        zero = jnp.zeros((rank, rank), bf16)

        def place(j, section, part, made):
            for level in range(levels):
                wide = [zero] * levels
                wide[level] = made(level)
                start = part * both + level * rank
                weights[j, section, start:start + rank, :] = jnp.concatenate(wide, axis=1)

        def spread(j, section, part, block):
            shape = (both, both)
            own_block = (
                lax.broadcasted_iota(jnp.int32, shape, 0) // rank
                == lax.broadcasted_iota(jnp.int32, shape, 1) // rank
            )
            weights[j, section, part * both:(part + 1) * both, :] = (
                jnp.where(own_block, block, 0.0).astype(bf16)
            )

        def doubled(block):
            return jnp.concatenate([block] * levels, axis=0)

        def gift(section, part):
            return gift_in[GIFTS.index((section, part))]

        def post(kept, slot, target):
            return remote(
                mail_out.at[kept], mail_in.at[slot], mail_send.at[slot], mail_recv.at[slot], g, target
            )

        mix_load.wait()
        perm_load.wait()
        lent[...] = joined(1, 1)
        index = lax.broadcasted_iota(jnp.int32, (rank, rank), 0)
        chosen = jnp.concatenate(
            [jnp.where(index == perm[level:level + 1, :], 1.0, 0.0) for level in range(levels)], axis=0
        ).astype(bf16)
        for part in range(2):
            spread(1, 0, part, jnp.dot(chosen, joined(0, part).astype(bf16), preferred_element_type=f32))
        place(1, 1, 0, factor_of(1, 0))
        own = project()
        for copy in leaf_loads:
            copy.start()
        row_load.wait()
        owner_load.wait()
        by_way(ahead_out)
        pl.semaphore_wait(barrier, 7 + jnp.where(bottom, 0, 2) + jnp.where(top, 2, 0))
        loans = [lend(0, gift_in.at[0]), lend(1, lent)]
        loans[1].start()
        pl.semaphore_signal(go, inc=1, device_id=(g, sibling), device_id_type=MESH)

        @pl.when(top)
        def _():
            for member in (b, sibling):
                pl.semaphore_signal(ready, inc=1, device_id=(up, member), device_id_type=MESH)

        @pl.when(jnp.logical_not(bottom))
        def _():
            hold(1).start()

        @pl.when(jnp.logical_not(top))
        def _():
            hold(0).start()

        gifts[0].wait_recv()
        loans[0].start()
        gifts[1].wait_recv()
        for part in range(2):
            spread(0, 0, part, jnp.dot(chosen, gift(0, part).astype(bf16), preferred_element_type=f32))
        spread(0, 1, 0, doubled(gift(1, 0)))
        seed.wait_recv()
        pair = [seed_in[...], own]
        state = [
            split_dot(jnp.concatenate([pair[j], pair[1 - j]], axis=1), weights[j, 0]) for j in range(2)
        ]

        raw, detour = post(RAW, RAW, second), post(RAW, DETOUR, cross)
        direct = post(DIRECT, DIRECT, third)
        for j in range(2):
            mail_out[RAW, j] = state[j]
        detour.start()
        mine = [split_dot(state[j], weights[j, 1, :both]) for j in range(2)]
        for j in range(2):
            mail_out[DIRECT, j] = mine[j]
        direct.start()
        raw.start()
        spread(0, 1, 1, doubled(gift(1, 1)))
        place(1, 1, 1, factor_of(1, 1))
        rest_load.wait()
        gifts[2].wait_recv()
        for section in (2, 3):
            for part in range(2):
                spread(0, section, part, doubled(gift(section, part)))
                place(1, section, part, factor_of(section, part))
        diagonals(0, 2)
        raw.wait_recv()
        state = [mine[j] + split_dot(mail_in[RAW, j], weights[j, 1, both:]) for j in range(2)]
        mine = [split_dot(state[j], weights[j, 2, :both]) for j in range(2)]
        detour.wait_recv()
        for j in range(2):
            loans[j].wait_recv()
            spread(j, sections, 0, doubled(borrowed[j]))
        far = [split_dot(mail_in[DETOUR, j], weights[j, sections, :both]) for j in range(2)]
        direct.wait_recv()
        state = [
            mine[j] + split_dot(mail_in[DIRECT, j] + far[j], weights[j, 2, both:]) for j in range(2)
        ]
        for j in range(2):
            mail_out[LAST, j] = state[j]
        last = post(LAST, LAST, fourth)
        last.start()
        mine = [split_dot(state[j], weights[j, 3, :both]) for j in range(2)]
        diagonals(2, leaves)
        lane_level = lax.broadcasted_iota(jnp.int32, (vectors, both), 1) // rank
        swapped = jnp.broadcast_to(owner[0:1, 0:1], (vectors, both)) != line
        to_half = lane_level == jnp.where(swapped, 1, 0)
        last.wait_recv()
        state = [mine[j] + split_dot(mail_in[LAST, j], weights[j, 3, both:]) for j in range(2)]

        told = [state[j].astype(bf16).astype(f32) for j in range(2)]
        ordered = [jnp.where(swapped, pltpu.roll(told[j], rank, 1), told[j]) for j in range(2)]
        for j in range(2):
            word_out[2 * j] = jnp.where(lane_level == 0, ordered[j], 0.0)
            word_out[2 * j + 1] = jnp.where(lane_level == 0, 0.0, ordered[j])
        word_out[4] = jnp.where(to_half, 0.0, told[0])
        sent = jnp.concatenate(
            [jnp.where(to_half, told[1], 0.0), jnp.where(to_half, 0.0, told[1])], axis=0
        ).astype(bf16)
        factor = row[...].reshape(both, rows)

        def make(c):
            block = jnp.dot(sent, factor[:, pieces[c]], preferred_element_type=f32)
            outgoing[c][0] = block[:vectors]
            outgoing[c][1] = block[vectors:]

        @pl.when(bottom)
        def _():
            word(4, g, sibling).start()

        @pl.when(jnp.logical_not(bottom))
        def _():
            word(1, down, sibling).start()
            word(3, down, b).start()

        word(0, half, sibling).start()

        @pl.when(jnp.logical_not(top))
        def _():
            word(2, half, b).start()

        make(1)

        @pl.when(jnp.logical_not(bottom))
        def _():
            shift(1, 1).start()

        @pl.when(jnp.logical_not(top))
        def _():
            shift(0, 1).start()

        @pl.when(bottom)
        def _():
            make(0)
            pl.semaphore_wait(ready, 1)
            for c in range(PIECES):
                shift(1, c).start()

        @pl.when(top)
        def _():
            make(0)
            for c, where in enumerate(pieces):
                shift(1, c).wait_recv()
                outgoing[c][0] += incoming[c][1]
                shift(0, c).start()
            for c in range(PIECES):
                inward(c, b).wait_recv()
                onward(c).start()
            for c, where in enumerate(pieces):
                shift(0, c).wait_recv()
                out_ref[:, where] += incoming[c][0]

        @pl.when(jnp.logical_not(top))
        def _():
            for way in (1, 0):
                give_ahead(way, b).wait_recv()
                narrow(way, ahead_in, ahead)
                word(2 + way, g, b).wait_recv()
            final = (word_in[2] + word_in[3]).astype(bf16)
            out_ref[:, :ahead] += jnp.dot(final, rows_low[:, :ahead], preferred_element_type=f32)
            for way in (1, 0):
                shift(way, 1).wait_recv()
            out_ref[:, ahead:] += incoming[1][0] + incoming[1][1]

        for copy in (*loans, raw, direct, detour, last):
            copy.wait_send()
        word(0, half, sibling).wait_send()
        for way in range(2):
            shift(way, 1).wait_send()

        @pl.when(bottom)
        def _():
            word(4, g, sibling).wait_send()
            shift(1, 0).wait_send()

        @pl.when(jnp.logical_not(bottom))
        def _():
            hold(1).wait_send()
            word(1, down, sibling).wait_send()
            word(3, down, b).wait_send()

        @pl.when(top)
        def _():
            shift(0, 0).wait_send()
            for c in range(PIECES):
                onward(c).wait_send()

        @pl.when(jnp.logical_not(top))
        def _():
            hold(0).wait_send()
            word(2, half, b).wait_send()


def shards(field, leaf_inverse, col_factor, row_factor, mixing, row_owner, rank_perm):
    vectors, rows = field.shape
    levels, rank, _ = col_factor.shape
    sections = mixing.shape[2]
    both = levels * rank
    ahead = rows * AHEAD[0] // AHEAD[1]
    f32, bf16 = jnp.float32, jnp.bfloat16
    args = (field, leaf_inverse, col_factor, row_factor, mixing, row_owner, rank_perm)
    args = [pltpu.with_memory_space_constraint(x, pltpu.HBM) for x in args]
    dma = pltpu.SemaphoreType.DMA
    return pl.pallas_call(
        kernel,
        out_shape=pltpu.VMEM((vectors, rows), f32),
        in_specs=[pl.BlockSpec(memory_space=pltpu.HBM)] * len(args),
        out_specs=pl.BlockSpec(memory_space=pltpu.VMEM),
        scratch_shapes=[
            pltpu.VMEM(field.shape, f32),
            pltpu.VMEM(leaf_inverse.shape, bf16),
            pltpu.VMEM(col_factor.shape, bf16),
            pltpu.VMEM(row_factor.shape, bf16),
            pltpu.VMEM(mixing.shape, bf16),
            pltpu.VMEM(row_owner.shape, jnp.int32),
            pltpu.VMEM(rank_perm.shape, jnp.int32),
            pltpu.VMEM((2, sections + 1, 2 * both, both), bf16),
            pltpu.VMEM((vectors, both), f32),
            pltpu.VMEM((vectors, both), f32),
            pltpu.VMEM((2 * sections, rank, both), f32),
            pltpu.VMEM((2 * sections, rank, both), f32),
            pltpu.VMEM((rank, both), f32),
            pltpu.VMEM((2, rank, both), f32),
            pltpu.VMEM((4, 2, vectors, both), f32),
            pltpu.VMEM((4, 2, vectors, both), f32),
            pltpu.VMEM((5, vectors, both), f32),
            pltpu.VMEM((5, vectors, both), f32),
            pltpu.VMEM((2, rank, rows), f32),
            pltpu.VMEM((2, rank, rows), f32),
            pltpu.VMEM((2, rank, ahead), f32),
            pltpu.VMEM((2, rank, ahead), f32),
            pltpu.VMEM((2, rank, ahead), f32),
            pltpu.VMEM((both, rows), bf16),
            pltpu.VMEM((2, vectors, ahead), f32),
            pltpu.VMEM((2, vectors, rows - ahead), f32),
            pltpu.VMEM((2, vectors, ahead), f32),
            pltpu.VMEM((2, vectors, rows - ahead), f32),
            pltpu.VMEM((vectors, ahead), f32),
            pltpu.VMEM((vectors, rows - ahead), f32),
            dma((7,)), dma((leaf_inverse.shape[0],)), dma((2,)), dma((3,)), dma((3,)),
            dma((2,)), dma((2,)), dma((4,)), dma((4,)), dma((5,)), dma((5,)), dma((2,)), dma((2,)), dma((2,)), dma((2,)),
            dma((2,)), dma((2,)),
            dma((2, PIECES)), dma((2, PIECES)), dma((PIECES,)), dma((PIECES,)),
            pltpu.SemaphoreType.REGULAR, pltpu.SemaphoreType.REGULAR,
        ],
        compiler_params=pltpu.CompilerParams(
            collective_id=0, has_side_effects=True, vmem_limit_bytes=60 * 2**20
        ),
    )(*args)


def solution(mesh):
    in_specs = (
        P(None, ("grp", "bf")),
        P(("grp", "bf"), None, None),
        P(None, None, ("grp", "bf")),
        P(None, None, ("grp", "bf")),
        P(("grp", "bf"), None, None, None, None, None),
        P(),
        P(),
    )
    out_specs = P(None, ("grp", "bf"))
    return jax.shard_map(shards, mesh=mesh, in_specs=in_specs, out_specs=out_specs, check_vma=False)
```

```python
import jax
import jax.numpy as jnp
from jax import lax
from jax.experimental import pallas as pl
from jax.experimental.pallas import tpu as pltpu
from jax.sharding import PartitionSpec as P

MESH = pl.DeviceIdType.MESH
AHEAD = 3, 8
PIECES = 2
STRIP = 16
RAW, DIRECT, DETOUR, LAST = range(4)
GIFTS = ((1, 1), (0, 0), (0, 1), (1, 0), (2, 0), (2, 1), (3, 0), (3, 1))


def split_dot(lhs, weights):
    high = lhs.astype(jnp.bfloat16)
    low = (lhs - high.astype(jnp.float32)).astype(jnp.bfloat16)
    both = jnp.dot(
        jnp.concatenate([high, low], axis=0), weights, preferred_element_type=jnp.float32
    )
    rows = lhs.shape[0]
    return both[:rows] + both[rows:]


def flip(index, bit):
    step = 2**bit
    return index + step - 2 * step * lax.rem(lax.div(index, step), 2)


def kernel(
    field_hbm, leaf_hbm, col_hbm, row_hbm, mix_hbm, owner_hbm, perm_hbm,
    out_ref,
    field, leaf, col, row, mix, owner, perm, weights,
    seed_out, seed_in, gift_out, gift_in, lent, borrowed, mail_out, mail_in,
    word_out, word_in, rows_out, rows_in, ahead_out, ahead_held, ahead_in, rows_low,
    out_first, out_rest, in_first, in_rest, relay_first, relay_rest,
    load_sem, leaf_sem, seed_sem, gift_send, gift_recv, lend_send, lend_recv, mail_send, mail_recv,
    word_send, word_recv, rows_send, rows_recv, held_send, held_recv, ahead_send, ahead_recv, shift_send, shift_recv, relay_send, relay_recv, ready, go,
):
    g, b = lax.axis_index("grp"), lax.axis_index("bf")
    groups = lax.axis_size("grp")
    vectors, rows = field.shape
    levels, rank, _ = col.shape
    leaves, order, _ = leaf.shape
    sections = mix.shape[2]
    both = levels * rank
    ahead = out_first.shape[2]
    pieces = (slice(0, ahead), slice(ahead, rows))
    outgoing, incoming, relay = (out_first, out_rest), (in_first, in_rest), (relay_first, relay_rest)
    f32, bf16 = jnp.float32, jnp.bfloat16

    def load(i, src, dst):
        copy = pltpu.make_async_copy(src, dst, load_sem.at[i])
        copy.start()
        return copy

    line, core = groups // 2, lax.rem(b, 2)
    z = lax.rem(g, line)
    half, down, up = lax.rem(g + line, groups), g - z + lax.rem(z + line - 1, line), g - z + lax.rem(z + 1, line)
    sibling, second, third, fourth = (flip(b, bit) for bit in range(4))
    cross = flip(second, 2)
    bottom, top = z == 0, z == line - 1
    barrier = pltpu.get_barrier_semaphore()

    def greet(group, member):
        pl.semaphore_signal(barrier, inc=1, device_id=(group, member), device_id_type=MESH)

    greet(half, b + 1 - core)

    @pl.when(jnp.logical_not(top))
    def _():
        greet(up, b + 1 - core)

    @pl.when(bottom)
    def _():
        greet(down, b + 1 - core)

    @pl.when(core == 1)
    def _():
        for friend in (third, fourth, second, cross):
            greet(g, friend)

    greet(g, sibling)
    half_mix = sections // 2
    mix_load = load(3, mix_hbm.at[:, :, :half_mix], mix.at[:, :, :half_mix])
    perm_load = load(2, perm_hbm, perm)
    field_load = load(0, field_hbm, field)
    col_load = load(1, col_hbm, col)
    rest_load = load(6, mix_hbm.at[:, :, half_mix:], mix.at[:, :, half_mix:])

    owner_load = load(5, owner_hbm, owner)
    row_load = load(4, row_hbm, row)
    leaf_loads = [
        pltpu.make_async_copy(leaf_hbm.at[n], leaf.at[n], leaf_sem.at[n]) for n in range(leaves)
    ]

    def remote(src, dst, send, recv, group, member):
        return pltpu.make_async_remote_copy(
            src_ref=src, dst_ref=dst, send_sem=send, recv_sem=recv,
            device_id=(group, member), device_id_type=MESH,
        )

    seed = remote(seed_out, seed_in, seed_sem.at[0], seed_sem.at[1], g, sibling)
    gifts = [
        remote(gift_out.at[part], gift_in.at[part], gift_send.at[i], gift_recv.at[i], g, sibling)
        for i, part in enumerate((pl.ds(0, 1), pl.ds(1, 3), pl.ds(4, 4)))
    ]

    def lend(j, source):
        return remote(source, borrowed.at[j], lend_send.at[j], lend_recv.at[j], g, third)

    def shift(way, c):
        return remote(
            outgoing[c].at[way], incoming[c].at[way], shift_send.at[way, c], shift_recv.at[way, c],
            (half, down)[way], b,
        )

    def inward(c, member):
        return remote(
            outgoing[c].at[1], relay[c], shift_send.at[1, c], relay_recv.at[c], down, member
        )

    def onward(c):
        return remote(
            relay[c], incoming[c].at[1], relay_send.at[c], shift_recv.at[1, c], half, sibling
        )

    def word(i, group, member):
        return remote(word_out.at[i], word_in.at[i], word_send.at[i], word_recv.at[i], group, member)

    def give_rows(way):
        return remote(
            rows_out.at[way], rows_in.at[way], rows_send.at[way], rows_recv.at[way],
            (half, down)[way], b,
        )

    def hold(way):
        return remote(
            ahead_out.at[way], ahead_held.at[way], held_send.at[way], held_recv.at[way], g, sibling
        )

    def give_ahead(way, member):
        return remote(
            ahead_held.at[way], ahead_in.at[way], ahead_send.at[way], ahead_recv.at[way],
            (half, down)[way], member,
        )

    def by_way(into):
        width = into.shape[2]
        swapped = jnp.broadcast_to(owner[0:1, 0:1], (STRIP, width)) != line

        def strip(i, carry):
            where = pl.ds(pl.multiple_of(i * STRIP, STRIP), STRIP)
            first, other = row[0, where, :width].astype(f32), row[1, where, :width].astype(f32)
            into[0, where] = jnp.where(swapped, other, first)
            into[1, where] = jnp.where(swapped, first, other)
            return carry

        lax.fori_loop(0, rank // STRIP, strip, 0)

    def narrow(way, source, width):
        def strip(i, carry):
            where = pl.ds(pl.multiple_of(i * STRIP, STRIP), STRIP)
            into = pl.ds(pl.multiple_of(way * rank + i * STRIP, STRIP), STRIP)
            rows_low[into, :width] = source[way, where].astype(bf16)
            return carry

        lax.fori_loop(0, rank // STRIP, strip, 0)

    def factor_of(section, part):
        return lambda level: mix[0, level, section, part]

    def joined(section, part):
        return jnp.concatenate([mix[0, level, section, part] for level in range(levels)], axis=1).astype(f32)

    def project():
        field_load.wait()
        col_load.wait()
        return lax.dot_general(
            field[...].astype(bf16), col[...].reshape(both, rows), (((1,), (1,)), ((), ())),
            preferred_element_type=f32,
        )

    def diagonal(n):
        pltpu.make_async_copy(leaf_hbm.at[n], leaf.at[n], leaf_sem.at[n]).wait()
        where = pl.ds(pl.multiple_of(n * order, order), order)
        out_ref[:, where] = jnp.dot(
            field[:, where].astype(bf16), leaf[n], preferred_element_type=f32
        )

    def diagonals(start, stop):
        def one(n, carry):
            diagonal(n)
            return carry

        lax.fori_loop(start, stop, one, 0)

    @pl.when(core == 0)
    def _():
        mix_load.wait()
        gift_out[0] = joined(*GIFTS[0])
        pl.semaphore_wait(barrier, 1)
        gifts[0].start()
        for i, (section, part) in enumerate(GIFTS[1:4], 1):
            gift_out[i] = joined(section, part)
        gifts[1].start()
        seed_out[...] = project()
        seed.start()
        for copy in leaf_loads:
            copy.start()
        rest_load.wait()
        for i, (section, part) in enumerate(GIFTS[4:], 4):
            gift_out[i] = joined(section, part)
        gifts[2].start()
        perm_load.wait()
        row_load.wait()
        owner_load.wait()
        by_way(rows_out)

        pl.semaphore_wait(go, 1)

        @pl.when(jnp.logical_not(bottom))
        def _():
            give_rows(1).start()

        give_rows(0).start()

        @pl.when(jnp.logical_not(bottom))
        def _():
            hold(1).wait_recv()
            give_ahead(1, sibling).start()

        @pl.when(jnp.logical_not(top))
        def _():
            hold(0).wait_recv()
            give_ahead(0, sibling).start()

        diagonals(0, leaves)

        @pl.when(bottom)
        def _():
            word(4, g, b).wait_recv()
            sent = word_in[4].astype(bf16)
            pl.semaphore_wait(ready, 1)
            for c, where in enumerate(pieces):
                outgoing[c][1] = jnp.dot(
                    sent, row[...].reshape(both, rows)[:, where], preferred_element_type=f32
                )
                inward(c, sibling).start()

        give_rows(0).wait_recv()
        narrow(0, rows_in, rows)

        @pl.when(top)
        def _():
            rows_low[rank:] = jnp.zeros((rank, rows), bf16)
            word_in[1] = jnp.zeros((vectors, both), f32)

        @pl.when(jnp.logical_not(top))
        def _():
            give_rows(1).wait_recv()
            narrow(1, rows_in, rows)
            word(1, g, b).wait_recv()

        word(0, g, b).wait_recv()
        final = (word_in[0] + word_in[1]).astype(bf16)
        out_ref[...] += jnp.dot(final, rows_low[...], preferred_element_type=f32)

        @pl.when(top)
        def _():
            for c, where in enumerate(pieces):
                shift(1, c).wait_recv()
                out_ref[:, where] += incoming[c][1]

        seed.wait_send()
        for gift in gifts:
            gift.wait_send()
        give_rows(0).wait_send()

        @pl.when(jnp.logical_not(bottom))
        def _():
            give_rows(1).wait_send()
            give_ahead(1, sibling).wait_send()

        @pl.when(jnp.logical_not(top))
        def _():
            give_ahead(0, sibling).wait_send()

        @pl.when(bottom)
        def _():
            for c in range(PIECES):
                inward(c, sibling).wait_send()

    @pl.when(core == 1)
    def _():
        zero = jnp.zeros((rank, rank), bf16)

        def place(j, section, part, made):
            for level in range(levels):
                wide = [zero] * levels
                wide[level] = made(level)
                start = part * both + level * rank
                weights[j, section, start:start + rank, :] = jnp.concatenate(wide, axis=1)

        def spread(j, section, part, block):
            shape = (both, both)
            own_block = (
                lax.broadcasted_iota(jnp.int32, shape, 0) // rank
                == lax.broadcasted_iota(jnp.int32, shape, 1) // rank
            )
            weights[j, section, part * both:(part + 1) * both, :] = (
                jnp.where(own_block, block, 0.0).astype(bf16)
            )

        def doubled(block):
            return jnp.concatenate([block] * levels, axis=0)

        def gift(section, part):
            return gift_in[GIFTS.index((section, part))]

        def post(kept, slot, target):
            return remote(
                mail_out.at[kept], mail_in.at[slot], mail_send.at[slot], mail_recv.at[slot], g, target
            )

        mix_load.wait()
        perm_load.wait()
        lent[...] = joined(1, 1)
        index = lax.broadcasted_iota(jnp.int32, (rank, rank), 0)
        chosen = jnp.concatenate(
            [jnp.where(index == perm[level:level + 1, :], 1.0, 0.0) for level in range(levels)], axis=0
        ).astype(bf16)
        for part in range(2):
            spread(1, 0, part, jnp.dot(chosen, joined(0, part).astype(bf16), preferred_element_type=f32))
        place(1, 1, 0, factor_of(1, 0))
        own = project()
        for copy in leaf_loads:
            copy.start()
        row_load.wait()
        owner_load.wait()
        by_way(ahead_out)
        pl.semaphore_wait(barrier, 7 + jnp.where(bottom, 0, 2) + jnp.where(top, 2, 0))
        loans = [lend(0, gift_in.at[0]), lend(1, lent)]
        pl.semaphore_signal(go, inc=1, device_id=(g, sibling), device_id_type=MESH)
        loans[1].start()

        @pl.when(top)
        def _():
            for member in (b, sibling):
                pl.semaphore_signal(ready, inc=1, device_id=(up, member), device_id_type=MESH)

        @pl.when(jnp.logical_not(bottom))
        def _():
            hold(1).start()

        @pl.when(jnp.logical_not(top))
        def _():
            hold(0).start()

        gifts[0].wait_recv()
        loans[0].start()
        gifts[1].wait_recv()
        for part in range(2):
            spread(0, 0, part, jnp.dot(chosen, gift(0, part).astype(bf16), preferred_element_type=f32))
        spread(0, 1, 0, doubled(gift(1, 0)))
        seed.wait_recv()
        pair = [seed_in[...], own]
        state = [
            split_dot(jnp.concatenate([pair[j], pair[1 - j]], axis=1), weights[j, 0]) for j in range(2)
        ]

        raw, detour = post(RAW, RAW, second), post(RAW, DETOUR, cross)
        direct = post(DIRECT, DIRECT, third)
        for j in range(2):
            mail_out[RAW, j] = state[j]
        detour.start()
        mine = [split_dot(state[j], weights[j, 1, :both]) for j in range(2)]
        for j in range(2):
            mail_out[DIRECT, j] = mine[j]
        direct.start()
        raw.start()
        spread(0, 1, 1, doubled(gift(1, 1)))
        place(1, 1, 1, factor_of(1, 1))
        rest_load.wait()
        gifts[2].wait_recv()
        for section in (2, 3):
            for part in range(2):
                spread(0, section, part, doubled(gift(section, part)))
                place(1, section, part, factor_of(section, part))
        diagonals(0, 2)
        raw.wait_recv()
        state = [mine[j] + split_dot(mail_in[RAW, j], weights[j, 1, both:]) for j in range(2)]
        mine = [split_dot(state[j], weights[j, 2, :both]) for j in range(2)]
        detour.wait_recv()
        for j in range(2):
            loans[j].wait_recv()
            spread(j, sections, 0, doubled(borrowed[j]))
        far = [split_dot(mail_in[DETOUR, j], weights[j, sections, :both]) for j in range(2)]
        direct.wait_recv()
        state = [
            mine[j] + split_dot(mail_in[DIRECT, j] + far[j], weights[j, 2, both:]) for j in range(2)
        ]
        for j in range(2):
            mail_out[LAST, j] = state[j]
        last = post(LAST, LAST, fourth)
        last.start()
        mine = [split_dot(state[j], weights[j, 3, :both]) for j in range(2)]
        diagonals(2, leaves)
        lane_level = lax.broadcasted_iota(jnp.int32, (vectors, both), 1) // rank
        swapped = jnp.broadcast_to(owner[0:1, 0:1], (vectors, both)) != line
        to_half = lane_level == jnp.where(swapped, 1, 0)
        last.wait_recv()
        state = [mine[j] + split_dot(mail_in[LAST, j], weights[j, 3, both:]) for j in range(2)]

        told = [state[j].astype(bf16).astype(f32) for j in range(2)]
        ordered = [jnp.where(swapped, pltpu.roll(told[j], rank, 1), told[j]) for j in range(2)]
        for j in range(2):
            word_out[2 * j] = jnp.where(lane_level == 0, ordered[j], 0.0)
            word_out[2 * j + 1] = jnp.where(lane_level == 0, 0.0, ordered[j])
        word_out[4] = jnp.where(to_half, 0.0, told[0])
        sent = jnp.concatenate(
            [jnp.where(to_half, told[1], 0.0), jnp.where(to_half, 0.0, told[1])], axis=0
        ).astype(bf16)
        factor = row[...].reshape(both, rows)

        def make(c):
            block = jnp.dot(sent, factor[:, pieces[c]], preferred_element_type=f32)
            outgoing[c][0] = block[:vectors]
            outgoing[c][1] = block[vectors:]

        @pl.when(bottom)
        def _():
            word(4, g, sibling).start()

        @pl.when(jnp.logical_not(bottom))
        def _():
            word(1, down, sibling).start()
            word(3, down, b).start()

        word(0, half, sibling).start()

        @pl.when(jnp.logical_not(top))
        def _():
            word(2, half, b).start()

        make(1)

        @pl.when(jnp.logical_not(bottom))
        def _():
            shift(1, 1).start()

        @pl.when(jnp.logical_not(top))
        def _():
            shift(0, 1).start()

        @pl.when(bottom)
        def _():
            make(0)
            pl.semaphore_wait(ready, 1)
            for c in range(PIECES):
                shift(1, c).start()

        @pl.when(top)
        def _():
            make(0)
            for c, where in enumerate(pieces):
                shift(1, c).wait_recv()
                outgoing[c][0] += incoming[c][1]
                shift(0, c).start()
            for c in range(PIECES):
                inward(c, b).wait_recv()
                onward(c).start()
            for c, where in enumerate(pieces):
                shift(0, c).wait_recv()
                out_ref[:, where] += incoming[c][0]

        @pl.when(jnp.logical_not(top))
        def _():
            for way in (1, 0):
                give_ahead(way, b).wait_recv()
                narrow(way, ahead_in, ahead)
                word(2 + way, g, b).wait_recv()
            final = (word_in[2] + word_in[3]).astype(bf16)
            out_ref[:, :ahead] += jnp.dot(final, rows_low[:, :ahead], preferred_element_type=f32)
            for way in (1, 0):
                shift(way, 1).wait_recv()
            out_ref[:, ahead:] += incoming[1][0] + incoming[1][1]

        for copy in (*loans, raw, direct, detour, last):
            copy.wait_send()
        word(0, half, sibling).wait_send()
        for way in range(2):
            shift(way, 1).wait_send()

        @pl.when(bottom)
        def _():
            word(4, g, sibling).wait_send()
            shift(1, 0).wait_send()

        @pl.when(jnp.logical_not(bottom))
        def _():
            hold(1).wait_send()
            word(1, down, sibling).wait_send()
            word(3, down, b).wait_send()

        @pl.when(top)
        def _():
            shift(0, 0).wait_send()
            for c in range(PIECES):
                onward(c).wait_send()

        @pl.when(jnp.logical_not(top))
        def _():
            hold(0).wait_send()
            word(2, half, b).wait_send()


def shards(field, leaf_inverse, col_factor, row_factor, mixing, row_owner, rank_perm):
    vectors, rows = field.shape
    levels, rank, _ = col_factor.shape
    sections = mixing.shape[2]
    both = levels * rank
    ahead = rows * AHEAD[0] // AHEAD[1]
    f32, bf16 = jnp.float32, jnp.bfloat16
    args = (field, leaf_inverse, col_factor, row_factor, mixing, row_owner, rank_perm)
    args = [pltpu.with_memory_space_constraint(x, pltpu.HBM) for x in args]
    dma = pltpu.SemaphoreType.DMA
    return pl.pallas_call(
        kernel,
        out_shape=pltpu.VMEM((vectors, rows), f32),
        in_specs=[pl.BlockSpec(memory_space=pltpu.HBM)] * len(args),
        out_specs=pl.BlockSpec(memory_space=pltpu.VMEM),
        scratch_shapes=[
            pltpu.VMEM(field.shape, f32),
            pltpu.VMEM(leaf_inverse.shape, bf16),
            pltpu.VMEM(col_factor.shape, bf16),
            pltpu.VMEM(row_factor.shape, bf16),
            pltpu.VMEM(mixing.shape, bf16),
            pltpu.VMEM(row_owner.shape, jnp.int32),
            pltpu.VMEM(rank_perm.shape, jnp.int32),
            pltpu.VMEM((2, sections + 1, 2 * both, both), bf16),
            pltpu.VMEM((vectors, both), f32),
            pltpu.VMEM((vectors, both), f32),
            pltpu.VMEM((2 * sections, rank, both), f32),
            pltpu.VMEM((2 * sections, rank, both), f32),
            pltpu.VMEM((rank, both), f32),
            pltpu.VMEM((2, rank, both), f32),
            pltpu.VMEM((4, 2, vectors, both), f32),
            pltpu.VMEM((4, 2, vectors, both), f32),
            pltpu.VMEM((5, vectors, both), f32),
            pltpu.VMEM((5, vectors, both), f32),
            pltpu.VMEM((2, rank, rows), f32),
            pltpu.VMEM((2, rank, rows), f32),
            pltpu.VMEM((2, rank, ahead), f32),
            pltpu.VMEM((2, rank, ahead), f32),
            pltpu.VMEM((2, rank, ahead), f32),
            pltpu.VMEM((both, rows), bf16),
            pltpu.VMEM((2, vectors, ahead), f32),
            pltpu.VMEM((2, vectors, rows - ahead), f32),
            pltpu.VMEM((2, vectors, ahead), f32),
            pltpu.VMEM((2, vectors, rows - ahead), f32),
            pltpu.VMEM((vectors, ahead), f32),
            pltpu.VMEM((vectors, rows - ahead), f32),
            dma((7,)), dma((leaf_inverse.shape[0],)), dma((2,)), dma((3,)), dma((3,)),
            dma((2,)), dma((2,)), dma((4,)), dma((4,)), dma((5,)), dma((5,)), dma((2,)), dma((2,)), dma((2,)), dma((2,)),
            dma((2,)), dma((2,)),
            dma((2, PIECES)), dma((2, PIECES)), dma((PIECES,)), dma((PIECES,)),
            pltpu.SemaphoreType.REGULAR, pltpu.SemaphoreType.REGULAR,
        ],
        compiler_params=pltpu.CompilerParams(
            collective_id=0, has_side_effects=True, vmem_limit_bytes=60 * 2**20
        ),
    )(*args)


def solution(mesh):
    in_specs = (
        P(None, ("grp", "bf")),
        P(("grp", "bf"), None, None),
        P(None, None, ("grp", "bf")),
        P(None, None, ("grp", "bf")),
        P(("grp", "bf"), None, None, None, None, None),
        P(),
        P(),
    )
    out_specs = P(None, ("grp", "bf"))
    return jax.shard_map(shards, mesh=mesh, in_specs=in_specs, out_specs=out_specs, check_vma=False)
```
